1024 devices in a mesh: blk: 64 (over y_lo, z), grp: 16 (over y_hi, x, core).
Axes of the slice: x: 4, y: 8 (y_hi: 2, y_lo: 4; y = y_hi * 4 + y_lo), z: 16, core: 2. Of those that a mesh axis runs over, the one named last changes fastest.
Arguments:
- embed: bfloat16 [16384, 256], P('blk'), may hold values from -1.5 to 1.5
- state: float32 [16384], P('blk'), may hold values from 0.01 to 1
- relation: float32 [512, 256], replicated, may hold values from -4 to 4
- src_index: int32 [64, 16, 4, 2, 128], P('blk', 'grp'), may hold values from 0 to 255
- dst_index: int32 [64, 16, 4, 2, 128], P('blk', 'grp'), may hold values from 0 to 255
- rel_index: int32 [64, 16, 4, 2, 128], P('blk', 'grp'), may hold values from 0 to 511
- neg_index: int32 [64, 16, 4, 2, 128], P('blk', 'grp'), may hold values from 0 to 255
- counts: int32 [64, 16, 4], P('blk', 'grp'), may hold values from 1 to 2
Outputs:
- new_embed: float32 [16384, 256], P(('blk', 'grp'))
- new_state: float32 [16384], P(('blk', 'grp'))
- dest_grad: float32 [16384, 256], P(('blk', 'grp'))
- rel_grad: float32 [512, 256], replicated
The draws below stay inside these ranges and needn't reach their ends.
Inputs may be any that keep to these rules, and one draw needn't show every extreme that they name: `counts`: blocks at and after the count are unused.
All inputs are finite; a program needn't handle non-finite values.
Results may differ from the reference program's by a relative error of at most 0.00043.
Values may be sent and summed in bfloat16 or wider, within the bound.
A program may use at most 32 MiB of HBM per device.

```python
import math
import jax
import jax.numpy as jnp
from jax import lax

D = 256
R = 512
SLAB = 256
BLOCKS = 2
EDGE = 128
NEG = 128
STEPS = 4
ENT = 16384
N_BLK = 64
N_GRP = 16


def set_ends(entries, stream_key, low, high):
    dims = entries.shape
    spot = [jax.random.randint(jax.random.fold_in(stream_key, axis), (), 0, dims[axis]) for axis in range(len(dims))]
    entries = entries.at[tuple(spot)].set(low)
    longest = dims.index(max(dims))
    spot[longest] = (spot[longest] + 1) % dims[longest]
    return entries.at[tuple(spot)].set(high)


def steps_of(own_key, extent, pieces, smallest, largest):
    def one(axis_at, parts):
        heights = jax.random.uniform(jax.random.fold_in(jax.random.fold_in(own_key, 6), axis_at), (parts,), jnp.float32, smallest / len(pieces), largest / len(pieces))
        return jnp.repeat(jnp.exp(heights), extent[axis_at] // parts).reshape((-1,) + (1,) * (len(extent) - axis_at - 1))

    level = one(*pieces[0])
    for cut in pieces[1:]:
        level = level * one(*cut)
    return level


def normal_values(key, extent, deviation, reach, pieces=(), held_as=jnp.bfloat16):
    values = jax.random.normal(key, extent, jnp.float32) * deviation
    if len(pieces) > 0:
        values = steps_of(key, extent, pieces, -0.22, 0.18) * values
    return jnp.clip(values, min=-reach, max=reach).astype(held_as)


def setup_inputs(seed: int = 0) -> dict:
    key_list = jax.random.split(jax.random.key(seed), 9)
    return {
        "embed": normal_values(key_list[0], (ENT, D), 0.25, 1.5, ((0, 64),)),
        "state": jnp.clip(jnp.exp(math.log(1.0) - 4.6051702 * jax.random.uniform(key_list[1], (ENT,), jnp.float32) ** steps_of(key_list[1], (ENT,), ((0, 64),), -0.2, 0.2)), 0.01, 1.0),
        "relation": normal_values(key_list[2], (R, D), 1.0, 4.0, (), jnp.float32),
        "src_index": set_ends(jax.random.randint(key_list[3], (N_BLK, N_GRP, STEPS, BLOCKS, EDGE), 0, SLAB), jax.random.fold_in(key_list[3], 1), 0, SLAB - 1).astype(jnp.int32),
        "dst_index": set_ends(jax.random.randint(key_list[4], (N_BLK, N_GRP, STEPS, BLOCKS, EDGE), 0, SLAB), jax.random.fold_in(key_list[4], 1), 0, SLAB - 1).astype(jnp.int32),
        "rel_index": set_ends(jax.random.randint(key_list[5], (N_BLK, N_GRP, STEPS, BLOCKS, EDGE), 0, R), jax.random.fold_in(key_list[5], 1), 0, R - 1).astype(jnp.int32),
        "neg_index": set_ends(jax.random.randint(key_list[6], (N_BLK, N_GRP, STEPS, BLOCKS, NEG), 0, SLAB), jax.random.fold_in(key_list[6], 1), 0, SLAB - 1).astype(jnp.int32),
        "counts": set_ends(jax.random.randint(key_list[7], (N_BLK, N_GRP, STEPS), 1, BLOCKS + 1), jax.random.fold_in(key_list[7], 1), 1, BLOCKS).astype(jnp.int32),
    }


def bucket(source_slab, target_slab, relation, src_rows, dst_rows, rel_rows, neg_rows, live_count):
    source = source_slab[src_rows].astype(jnp.float32)
    target = target_slab[dst_rows].astype(jnp.float32)
    negatives = target_slab[neg_rows].astype(jnp.float32)
    rel_vals = relation[rel_rows]
    live_mask = (jnp.arange(BLOCKS, dtype=jnp.int32) < live_count).astype(jnp.float32)
    scaled = source * rel_vals
    positive = lax.optimization_barrier(jnp.sum(scaled * target, axis=-1))
    scaled_b = scaled.astype(jnp.bfloat16).astype(jnp.float32)
    negative = jnp.einsum('bed,bnd->ben', scaled_b, negatives)
    pos_grad = -jax.nn.sigmoid(-positive) * live_mask[:, None]
    neg_grad = (jax.nn.sigmoid(negative) * (live_mask[:, None, None] / NEG)).astype(jnp.bfloat16).astype(jnp.float32)
    scaled_grad = pos_grad[..., None] * target + jnp.einsum('ben,bnd->bed', neg_grad, negatives)
    source_g = (scaled_grad * rel_vals).reshape(-1, D)
    rel_g = (scaled_grad * source).reshape(-1, D)
    target_g = (pos_grad[..., None] * scaled).reshape(-1, D)
    neg_g = jnp.einsum('ben,bed->bnd', neg_grad, scaled_b).reshape(-1, D)
    src_total = jnp.zeros((SLAB, D), jnp.float32).at[src_rows.reshape(-1)].add(source_g)
    dst_total = jnp.zeros((SLAB, D), jnp.float32).at[dst_rows.reshape(-1)].add(target_g)
    dst_total = dst_total.at[neg_rows.reshape(-1)].add(neg_g)
    rel_total = jnp.zeros((R, D), jnp.float32).at[rel_rows.reshape(-1)].add(rel_g)
    return (src_total, dst_total, rel_total)

def reference(embed, state, relation, src_index, dst_index, rel_index, neg_index, counts):
    total_turns = N_BLK * N_GRP * STEPS

    def one_turn(turn, carry):
        src_all, dst_all, rel_all = carry
        owner = turn // (N_GRP * STEPS)
        member = turn // STEPS % N_GRP
        cycle_step = turn % STEPS
        other = (owner - cycle_step + N_BLK) % N_BLK
        source_slab = lax.dynamic_slice_in_dim(embed, (owner * SLAB).astype(jnp.int32), SLAB, 0)
        target_slab = lax.dynamic_slice_in_dim(embed, (other * SLAB).astype(jnp.int32), SLAB, 0)
        src_part, dst_part, rel_part = bucket(source_slab, target_slab, relation, src_index[owner, member, cycle_step], dst_index[owner, member, cycle_step], rel_index[owner, member, cycle_step], neg_index[owner, member, cycle_step], counts[owner, member, cycle_step])
        src_old = lax.dynamic_slice_in_dim(src_all, (owner * SLAB).astype(jnp.int32), SLAB, 0)
        src_all = lax.dynamic_update_slice_in_dim(src_all, src_old + src_part, (owner * SLAB).astype(jnp.int32), 0)
        dst_old = lax.dynamic_slice_in_dim(dst_all, (other * SLAB).astype(jnp.int32), SLAB, 0)
        dst_all = lax.dynamic_update_slice_in_dim(dst_all, dst_old + dst_part, (other * SLAB).astype(jnp.int32), 0)
        return (src_all, dst_all, rel_all + rel_part)
    start_carry = (jnp.zeros((ENT, D), jnp.float32), jnp.zeros((ENT, D), jnp.float32), jnp.zeros((R, D), jnp.float32))
    src_all, dst_all, rel_grad = lax.fori_loop(0, total_turns, one_turn, start_carry)
    new_state = state + lax.optimization_barrier(jnp.mean(src_all * src_all, axis=-1))
    new_embed = embed.astype(jnp.float32) - 0.5 * src_all / jnp.sqrt(new_state)[:, None]
    dest_grad = jnp.roll(dst_all.reshape(N_BLK, SLAB, D), STEPS - 1, axis=0).reshape(ENT, D)
    return (new_embed, new_state, dest_grad, rel_grad)
```

```python
import functools

import jax
import jax.numpy as jnp
from jax import lax
from jax.experimental import pallas as pl
from jax.experimental.pallas import tpu as pltpu
from jax.sharding import PartitionSpec as P

NZ = 16
NX = 4
NY = 8
NB = 64
MESH = pl.DeviceIdType.MESH
F32 = jnp.float32
BF16 = jnp.bfloat16


def position():
    b = lax.axis_index("blk")
    g = lax.axis_index("grp")
    z = lax.rem(b, NZ)
    y = lax.div(g, 8) * 4 + lax.div(b, NZ)
    x = lax.rem(lax.div(g, 2), NX)
    c = lax.rem(g, 2)
    return b, g, z, y, x, c


def at(z, y, x, c):
    return (lax.rem(y, 4) * NZ + z, lax.div(y, 4) * 8 + x * 2 + c)


def remote(src, dst, send, recv, where):
    return pltpu.make_async_remote_copy(
        src_ref=src, dst_ref=dst, send_sem=send, recv_sem=recv, device_id=where, device_id_type=MESH
    )


def greet(where):
    pl.semaphore_signal(pltpu.get_barrier_semaphore(), inc=1, device_id=where, device_id_type=MESH)


def exchange_kernel(
    embed, src, dst, rel, neg, counts, slab, index, packed, idx_send, idx_recv, slab_send, slab_recv
):
    b, g, z, y, x, c = position()
    sibling = (b, g + 1 - 2 * c)
    ahead = (lax.rem(b + x, NB), g)
    behind = (lax.rem(b + NB - x, NB), g)
    greet(sibling)
    for d in range(1, NX):
        greet(at(z, y, lax.rem(x + d, NX), c))

    @pl.when(x > 0)
    def _():
        greet(ahead)
        greet(behind)

    for t in range(NX):
        blocks = lax.broadcasted_iota(jnp.int32, (2, 128), 0)
        packed[t, 0:2] = jnp.where(blocks < counts[0, 0, t], src[0, 0, t], -1)
        packed[t, 2:4] = dst[0, 0, t]
        packed[t, 4:6] = rel[0, 0, t]
        packed[t, 6:8] = neg[0, 0, t]
    pl.semaphore_wait(pltpu.get_barrier_semaphore(), jnp.where(x > 0, NX + 2, NX))

    half = pl.ds(pl.multiple_of(c * 128, 128), 128)
    other = pl.ds(pl.multiple_of((1 - c) * 128, 128), 128)

    @pl.when(x > 0)
    def _():
        remote(embed.at[half], slab.at[half], slab_send.at[0], slab_recv.at[0], ahead).start()

    sends = []
    for d in (2, 1, 3):
        there = lax.rem(x + d, NX)
        copy = remote(
            packed.at[there], index.at[x], idx_send.at[d - 1], idx_recv.at[d - 1], at(z, y, there, c)
        )
        copy.start()
        sends.append(copy)
    index[pl.ds(x, 1)] = packed[pl.ds(x, 1)]

    @pl.when(x == 0)
    def _():
        slab[...] = embed[...]

    @pl.when(x > 0)
    def _():
        first = remote(embed.at[half], slab.at[half], slab_send.at[0], slab_recv.at[0], ahead)
        second = remote(slab.at[half], slab.at[half], slab_send.at[1], slab_recv.at[1], sibling)
        first.wait_recv()
        second.start()
        first.wait_send()
        second.wait_send()
        remote(slab.at[other], slab.at[other], slab_send.at[1], slab_recv.at[1], sibling).wait_recv()

    for copy in sends:
        copy.wait()


def compute_kernel(
    index, source, slab, relation, src_out, dst_out, rel_out, parts, hot_src, hot_dst, hot_rel, g_src, g_dst, g_rel
):
    r = relation[...]
    high = r.astype(BF16)
    rest = r - high.astype(F32)
    mid = rest.astype(BF16)
    parts[:, 0:256] = high
    parts[:, 256:512] = mid
    parts[:, 512:768] = (rest - mid.astype(F32)).astype(BF16)

    def hot(hit):
        return jnp.where(hit, 1.0, 0.0).astype(BF16)

    def split(ref, rows, value):
        top = value.astype(BF16)
        ref[rows, 0:256] = top
        ref[rows, 256:512] = (value - top.astype(F32)).astype(BF16)

    def dot(a, b):
        return jnp.dot(a, b, preferred_element_type=F32)

    lane = lax.broadcasted_iota(jnp.int32, (256, 256), 1)
    lane_r = lax.broadcasted_iota(jnp.int32, (256, 512), 1)
    sub = lax.broadcasted_iota(jnp.int32, (256, 256), 0)
    sub_r = lax.broadcasted_iota(jnp.int32, (512, 256), 0)
    for k in range(NX):
        rows = index[k]
        columns = rows.T

        def row(i):
            return jnp.concatenate([rows[2 * i : 2 * i + 1], rows[2 * i + 1 : 2 * i + 2]], axis=1)

        def column(i):
            return jnp.concatenate([columns[:, 2 * i : 2 * i + 1], columns[:, 2 * i + 1 : 2 * i + 2]], axis=0)

        edges = slice(k * 256, k * 256 + 256)
        negs = slice(1024 + k * 256, 1024 + k * 256 + 256)
        hot_src[:, edges] = hot(sub == row(0))
        hot_dst[:, edges] = hot(sub == row(1))
        hot_dst[:, negs] = hot(sub == row(3))
        hot_rel[:, edges] = hot(sub_r == row(2))
        src_v = dot(hot(lane == column(0)), source[...])
        dst_v = dot(hot(lane == column(1)), slab[...])
        neg_v = dot(hot(lane == column(3)), slab[...]).astype(BF16)
        pieces = dot(hot(lane_r == column(2)), parts[...])
        rel_v = (pieces[:, 0:256] + pieces[:, 256:512]) + pieces[:, 512:768]
        scaled = src_v * rel_v
        positive = jnp.sum(scaled * dst_v, axis=1, keepdims=True)
        pos_grad = -jax.nn.sigmoid(-positive)
        scaled_b = scaled.astype(BF16)
        from_neg = []
        neg_g = []
        for j in range(2):
            block = slice(j * 128, j * 128 + 128)
            s, n = scaled_b[block], neg_v[block]
            score = lax.dot_general(s, n, (((1,), (1,)), ((), ())), preferred_element_type=F32)
            weight = (jax.nn.sigmoid(score) * (1.0 / 128.0)).astype(BF16)
            from_neg.append(dot(weight, n))
            neg_g.append(lax.dot_general(weight, s, (((0,), (0,)), ((), ())), preferred_element_type=F32))
        scaled_grad = pos_grad * dst_v + jnp.concatenate(from_neg, axis=0)
        split(g_rel, edges, scaled_grad * src_v)
        split(g_src, edges, scaled_grad * rel_v)
        split(g_dst, edges, pos_grad * scaled)
        split(g_dst, negs, jnp.concatenate(neg_g, axis=0))

    def total(h, g):
        both = dot(h[...], g[...])
        return both[:, 0:256] + both[:, 256:512]

    rel_out[...] = total(hot_rel, g_rel).reshape(rel_out.shape)
    src_out[...] = total(hot_src, g_src).reshape(src_out.shape)
    dst_out[...] = total(hot_dst, g_dst).reshape(dst_out.shape)


def reduce_kernel(
    rel_in,
    src_in,
    dst_in,
    embed,
    state,
    new_embed,
    new_state,
    dest_out,
    rel_out,
    rel_pair,
    src_pair,
    dst_pair,
    rel_xy,
    rel_z,
    src_x,
    dst_x,
    src_half,
    src_y,
    dst_y,
    send,
    recv,
    dst_send,
    dst_recv,
):
    b, g, z, y, x, c = position()
    sibling = (b, g + 1 - 2 * c)
    opposite = at(z, lax.rem(y + 4, NY), x, c)
    yh = lax.div(y, 4)
    base = lax.rem(b + 3 + NB - x, NB)
    row_of = lax.div(g, 8) * 8 + c
    mine = x * NY + y

    offsets = [(dx, dy) for dx in (2, 1, 3, 0) for dy in (4, 3, 5, 2, 6, 1, 7, 0) if (dx, dy) != (0, 0)]
    z_offsets = (8, 7, 9, 6, 10, 5, 11, 4, 12, 3, 13, 2, 14, 1, 15)

    def plane(dx, dy):
        px, py = lax.rem(x + dx, NX), lax.rem(y + dy, NY)
        return px * NY + py, at(z, py, px, c)

    greet(sibling)
    for dz in z_offsets:
        greet(at(lax.rem(z + dz, NZ), y, x, c))
    for dx, dy in offsets:
        greet(plane(dx, dy)[1])
    for t in range(NX):
        to = (base, row_of + 2 * t)
        source = (lax.rem(b + NB - 3 + t, NB), row_of + 2 * t)

        @pl.when(jnp.logical_or(x != 3, t != 3))
        def _():
            greet(to)
            greet(source)

    pl.semaphore_wait(pltpu.get_barrier_semaphore(), 1 + 15 + 31 + jnp.where(x == 3, 6, 8))

    def pair(source, target, i):
        return remote(source, target, send.at[i], recv.at[i], sibling)

    rel_c = pair(rel_in.at[1 - c], rel_pair, 0)
    src_c = pair(src_in.at[:, :, 1 - c], src_pair, 1)
    dst_c = pair(dst_in.at[:, :, 1 - c], dst_pair, 2)
    rel_c.start()
    src_c.start()
    dst_c.start()

    rel_c.wait()
    rel_pair[...] = rel_pair[...] + rel_in[pl.ds(c, 1)][0]
    for i, (dx, dy) in enumerate(offsets):
        chunk, where = plane(dx, dy)
        remote(rel_pair.at[chunk], rel_xy.at[i], send.at[3], recv.at[3], where).start()

    src_c.wait()
    src_pair[...] = src_pair[...] + src_in[:, :, pl.ds(c, 1)].reshape(2, 4, 16, 256)
    src_sends = []
    for d in (2, 1, 3):
        px = lax.rem(x + d, NX)
        copy = remote(src_pair.at[:, px], src_x.at[d], send.at[4 + d], recv.at[4 + d], at(z, y, px, c))
        copy.start()
        src_sends.append(copy)
    dst_c.wait()
    dst_pair[...] = dst_pair[...] + dst_in[:, :, pl.ds(c, 1)].reshape(2, 4, 16, 256)
    for t in range(NX):
        to = (base, row_of + 2 * t)

        @pl.when(jnp.logical_or(x != 3, t != 3))
        def _():
            remote(dst_pair.at[:, t], dst_x.at[x], dst_send.at[t], dst_recv.at[x], to).start()

    @pl.when(x == 3)
    def _():
        dst_x[3] = dst_pair[:, 3]

    def chunks(ref, n, sem):
        return pltpu.make_async_copy(ref.at[pl.ds(0, n)], ref.at[pl.ds(0, n)], sem)

    chunks(rel_xy, 31, recv.at[3]).wait()
    own = rel_pair[pl.ds(mine, 1)][0] + jnp.sum(rel_xy[...], axis=0)
    rel_z[pl.ds(z, 1)] = own[None]
    for dz in z_offsets:
        where = at(lax.rem(z + dz, NZ), y, x, c)
        remote(rel_z.at[z], rel_z.at[z], send.at[8], recv.at[8], where).start()

    for copy in src_sends:
        copy.wait_recv()
    src_half[...] = (src_pair[:, pl.ds(x, 1)].reshape(2, 16, 256) + src_x[1]) + (src_x[2] + src_x[3])
    src_far = remote(src_half.at[1 - yh], src_y, send.at[9], recv.at[9], opposite)
    src_far.start()
    for t in range(NX):
        source = (lax.rem(b + NB - 3 + t, NB), row_of + 2 * t)

        @pl.when(jnp.logical_or(x != 3, t != 3))
        def _():
            remote(dst_pair.at[:, t], dst_x.at[t], dst_send.at[t], dst_recv.at[t], source).wait_recv()

    dst_x[0] = (dst_x[0] + dst_x[1]) + (dst_x[2] + dst_x[3])
    dst_far = remote(dst_x.at[0, 1 - yh], dst_y, send.at[10], recv.at[10], opposite)
    dst_far.start()

    src_far.wait_recv()
    total = src_half[pl.ds(yh, 1)][0] + src_y[...]
    lane = lax.broadcasted_iota(jnp.int32, (16, 256), 1)
    line = lax.broadcasted_iota(jnp.int32, (16, 256), 0)
    old = jnp.sum(jnp.where(lane == line + g * 16, state[...], 0.0), axis=1, keepdims=True)
    fresh = old + jnp.sum(total * total, axis=1, keepdims=True) * (1.0 / 256.0)
    own_rows = embed[pl.ds(pl.multiple_of(g * 16, 16), 16)].astype(F32)
    new_embed[...] = own_rows - 0.5 * total / jnp.sqrt(fresh)
    lane16 = lax.broadcasted_iota(jnp.int32, (16, 16), 1)
    line16 = lax.broadcasted_iota(jnp.int32, (16, 16), 0)
    new_state[...] = jnp.sum(jnp.where(lane16 == line16, fresh, 0.0), axis=0, keepdims=True)
    dst_far.wait_recv()
    dest_out[...] = dst_x[0, pl.ds(yh, 1)].reshape(16, 256) + dst_y[...]

    chunks(rel_z, 15, recv.at[8]).wait()
    rel_out[pl.ds(c, 1), pl.ds(mine, 1)] = jnp.sum(rel_z[...], axis=0)[None, None]
    for dx, dy in offsets:
        _, where = plane(dx, dy)
        remote(rel_out.at[c, mine], rel_out.at[c, mine], send.at[11], recv.at[11], where).start()
    chunks(rel_xy, 31, recv.at[11]).wait()
    last = remote(rel_out.at[c], rel_out.at[c], send.at[12], recv.at[12], sibling)
    last.start()
    chunks(rel_xy, 31, send.at[3]).wait()
    chunks(rel_z, 15, send.at[8]).wait()
    chunks(rel_xy, 31, send.at[11]).wait()
    for copy in src_sends:
        copy.wait_send()
    for t in range(NX):

        @pl.when(jnp.logical_or(x != 3, t != 3))
        def _():
            remote(dst_pair.at[:, t], dst_x.at[x], dst_send.at[t], dst_recv.at[x], sibling).wait_send()

    src_far.wait_send()
    dst_far.wait_send()
    last.wait_send()
    remote(rel_out.at[1 - c], rel_out.at[1 - c], send.at[12], recv.at[12], sibling).wait_recv()


def on_device(embed, state, relation, src_index, dst_index, rel_index, neg_index, counts):
    vmem = pl.BlockSpec(memory_space=pltpu.VMEM)
    smem = pl.BlockSpec(memory_space=pltpu.SMEM)
    dma = pltpu.SemaphoreType.DMA

    def params(**more):
        return pltpu.CompilerParams(vmem_limit_bytes=48 << 20, **more)

    slab, index = pl.pallas_call(
        exchange_kernel,
        out_shape=[jax.ShapeDtypeStruct((256, 256), BF16), jax.ShapeDtypeStruct((4, 8, 128), jnp.int32)],
        in_specs=[vmem] * 5 + [smem],
        out_specs=[vmem] * 2,
        scratch_shapes=[pltpu.VMEM((4, 8, 128), jnp.int32), dma((3,)), dma((3,)), dma((2,)), dma((2,))],
        compiler_params=params(collective_id=0, has_side_effects=True),
        name="exchange",
    )(embed, src_index, dst_index, rel_index, neg_index, counts)
    src_sum, dst_sum, rel_sum = pl.pallas_call(
        compute_kernel,
        out_shape=[
            jax.ShapeDtypeStruct((2, 4, 2, 16, 256), F32),
            jax.ShapeDtypeStruct((2, 4, 2, 16, 256), F32),
            jax.ShapeDtypeStruct((2, 32, 8, 256), F32),
        ],
        in_specs=[vmem] * 4,
        out_specs=[vmem] * 3,
        scratch_shapes=[
            pltpu.VMEM((512, 768), BF16),
            pltpu.VMEM((256, 1024), BF16),
            pltpu.VMEM((256, 2048), BF16),
            pltpu.VMEM((512, 1024), BF16),
            pltpu.VMEM((1024, 512), BF16),
            pltpu.VMEM((2048, 512), BF16),
            pltpu.VMEM((1024, 512), BF16),
        ],
        compiler_params=params(),
        name="buckets",
    )(index, embed, slab, relation)
    new_embed, new_state, dest, rel_grad = pl.pallas_call(
        reduce_kernel,
        out_shape=[
            jax.ShapeDtypeStruct((16, 256), F32),
            jax.ShapeDtypeStruct((1, 16), F32),
            jax.ShapeDtypeStruct((16, 256), F32),
            jax.ShapeDtypeStruct((2, 32, 8, 256), F32),
        ],
        in_specs=[vmem] * 5,
        out_specs=[vmem] * 4,
        scratch_shapes=[
            pltpu.VMEM((32, 8, 256), F32),
            pltpu.VMEM((2, 4, 16, 256), F32),
            pltpu.VMEM((2, 4, 16, 256), F32),
            pltpu.VMEM((31, 8, 256), F32),
            pltpu.VMEM((16, 8, 256), F32),
            pltpu.VMEM((4, 2, 16, 256), F32),
            pltpu.VMEM((4, 2, 16, 256), F32),
            pltpu.VMEM((2, 16, 256), F32),
            pltpu.VMEM((16, 256), F32),
            pltpu.VMEM((16, 256), F32),
            dma((13,)),
            dma((13,)),
            dma((4,)),
            dma((4,)),
        ],
        compiler_params=params(collective_id=1, has_side_effects=True),
        name="reduce",
    )(rel_sum, src_sum, dst_sum, embed, state.reshape(1, 256))
    return (new_embed, new_state.reshape(16), dest, rel_grad.reshape(512, 256))


def solution(mesh):
    return jax.shard_map(
        on_device,
        mesh=mesh,
        in_specs=(
            P("blk", None),
            P("blk"),
            P(),
            P("blk", "grp", None, None, None),
            P("blk", "grp", None, None, None),
            P("blk", "grp", None, None, None),
            P("blk", "grp", None, None, None),
            P("blk", "grp", None),
        ),
        out_specs=(P(("blk", "grp"), None), P(("blk", "grp")), P(("blk", "grp"), None), P()),
        check_vma=False,
    )
```

```python
import jax
import jax.numpy as jnp
from jax import lax
from jax.experimental import pallas as pl
from jax.experimental.pallas import tpu as pltpu
from jax.sharding import PartitionSpec as P

NZ = 16
NX = 4
NY = 8
NB = 64
MESH = pl.DeviceIdType.MESH
F32 = jnp.float32
BF16 = jnp.bfloat16


def position():
    b = lax.axis_index("blk")
    g = lax.axis_index("grp")
    z = lax.rem(b, NZ)
    y = lax.div(g, 8) * 4 + lax.div(b, NZ)
    x = lax.rem(lax.div(g, 2), NX)
    c = lax.rem(g, 2)
    return b, g, z, y, x, c


def at(z, y, x, c):
    return (lax.rem(y, 4) * NZ + z, lax.div(y, 4) * 8 + x * 2 + c)


def remote(src, dst, send, recv, where):
    return pltpu.make_async_remote_copy(
        src_ref=src, dst_ref=dst, send_sem=send, recv_sem=recv, device_id=where, device_id_type=MESH
    )


def greet(where):
    pl.semaphore_signal(pltpu.get_barrier_semaphore(), inc=1, device_id=where, device_id_type=MESH)


def dot(a, b):
    return jnp.dot(a, b, preferred_element_type=F32)


def hot(hit):
    return jnp.where(hit, 1.0, 0.0).astype(BF16)


def columns_of(rows):
    turned = rows.T
    return jnp.concatenate([turned[:, 0:1], turned[:, 1:2]], axis=0)


def line_of(rows):
    return jnp.concatenate([rows[0:1], rows[1:2]], axis=1)


def exchange_kernel(
    embed,
    relation,
    src,
    dst,
    rel,
    neg,
    counts,
    slab,
    index,
    src_rows,
    rel_rows,
    hot_src,
    hot_dst,
    hot_rel,
    own,
    table,
    parts,
    loaded,
    live,
    packed,
    load_sem,
    idx_send,
    idx_recv,
    slab_send,
    slab_recv,
):
    b, g, z, y, x, c = position()
    loads = [pltpu.make_async_copy(ref.at[0, 0], loaded.at[i], load_sem.at[i]) for i, ref in enumerate((src, dst, rel, neg))]
    loads.append(pltpu.make_async_copy(counts.at[0], live, load_sem.at[4]))
    load_own = pltpu.make_async_copy(embed, own, load_sem.at[5])
    load_table = pltpu.make_async_copy(relation, table, load_sem.at[6])
    for copy in loads:
        copy.start()
    load_own.start()
    load_table.start()
    sibling = (b, g + 1 - 2 * c)
    ahead = (lax.rem(b + x, NB), g)
    behind = (lax.rem(b + NB - x, NB), g)
    greet(sibling)
    for d in range(1, NX):
        greet(at(z, y, lax.rem(x + d, NX), c))

    @pl.when(x > 0)
    def _():
        greet(ahead)
        greet(behind)

    for copy in loads:
        copy.wait()
    blocks = lax.broadcasted_iota(jnp.int32, (2, 128), 0)
    spots = lax.broadcasted_iota(jnp.int32, (1, 4), 1)
    for t in range(NX):
        count = jnp.sum(jnp.where(spots == t, live[...], 0), axis=1, keepdims=True)
        packed[t, 0] = jnp.where(blocks < count, loaded[0, t], -1)
        for i in range(1, 4):
            packed[t, i] = loaded[i, t]
    load_own.wait()
    pl.semaphore_wait(pltpu.get_barrier_semaphore(), jnp.where(x > 0, NX + 2, NX))

    half = pl.ds(pl.multiple_of(c * 128, 128), 128)
    other = pl.ds(pl.multiple_of((1 - c) * 128, 128), 128)

    sends = []
    for d in (2, 1, 3):
        there = lax.rem(x + d, NX)
        copy = remote(packed.at[there], index.at[x], idx_send.at[d - 1], idx_recv.at[d - 1], at(z, y, there, c))
        copy.start()
        sends.append(copy)

    @pl.when(x > 0)
    def _():
        remote(own.at[half], slab.at[half], slab_send.at[0], slab_recv.at[0], ahead).start()

    index[pl.ds(x, 1)] = packed[pl.ds(x, 1)]

    @pl.when(x == 0)
    def _():
        slab[...] = own[...]

    load_table.wait()
    r = table[...]
    high = r.astype(BF16)
    rest = r - high.astype(F32)
    middle = rest.astype(BF16)
    parts[:, 0:256] = high
    parts[:, 256:512] = middle
    parts[:, 512:768] = (rest - middle.astype(F32)).astype(BF16)
    for copy in sends:
        copy.wait()

    lane = lax.broadcasted_iota(jnp.int32, (256, 256), 1)
    lane_r = lax.broadcasted_iota(jnp.int32, (256, 512), 1)
    sub = lax.broadcasted_iota(jnp.int32, (256, 256), 0)
    sub_r = lax.broadcasted_iota(jnp.int32, (2, 256, 256), 0) * 256 + lax.broadcasted_iota(jnp.int32, (2, 256, 256), 1)
    for k in range(NX):
        edges = slice(k * 256, k * 256 + 256)
        negs = slice(1024 + k * 256, 1024 + k * 256 + 256)
        src_rows[edges] = dot(hot(lane == columns_of(index[k, 0])), own[...])
        pieces = dot(hot(lane_r == columns_of(index[k, 2])), parts[...])
        rel_rows[edges] = (pieces[:, 0:256] + pieces[:, 256:512]) + pieces[:, 512:768]
        hot_src[:, edges] = hot(sub == line_of(index[k, 0]))
        hot_dst[:, edges] = hot(sub == line_of(index[k, 1]))
        hot_dst[:, negs] = hot(sub == line_of(index[k, 3]))
        hot_rel[:, :, edges] = hot(sub_r == line_of(index[k, 2])[None])

    @pl.when(x > 0)
    def _():
        first = remote(own.at[half], slab.at[half], slab_send.at[0], slab_recv.at[0], ahead)
        second = remote(slab.at[half], slab.at[half], slab_send.at[1], slab_recv.at[1], sibling)
        first.wait_recv()
        second.start()
        first.wait_send()
        second.wait_send()
        remote(slab.at[other], slab.at[other], slab_send.at[1], slab_recv.at[1], sibling).wait_recv()


def bucket_gradients(index, slab, src_rows, rel_rows, g_src, g_dst, g_rel):
    def split(ref, rows, value):
        top = value.astype(BF16)
        ref[rows, 0:256] = top
        ref[rows, 256:512] = (value - top.astype(F32)).astype(BF16)

    lane = lax.broadcasted_iota(jnp.int32, (256, 256), 1)
    for k in range(NX):
        edges = slice(k * 256, k * 256 + 256)
        negs = slice(1024 + k * 256, 1024 + k * 256 + 256)
        src_v = src_rows[edges]
        rel_v = rel_rows[edges]
        dst_v = dot(hot(lane == columns_of(index[k, 1])), slab[...])
        neg_v = dot(hot(lane == columns_of(index[k, 3])), slab[...]).astype(BF16)
        scaled = src_v * rel_v
        positive = jnp.sum(scaled * dst_v, axis=1, keepdims=True)
        pos_grad = -jax.nn.sigmoid(-positive)
        scaled_b = scaled.astype(BF16)
        from_neg = []
        neg_g = []
        for j in range(2):
            block = slice(j * 128, j * 128 + 128)
            s, n = scaled_b[block], neg_v[block]
            score = lax.dot_general(s, n, (((1,), (1,)), ((), ())), preferred_element_type=F32)
            weight = (jax.nn.sigmoid(score) * (1.0 / 128.0)).astype(BF16)
            from_neg.append(dot(weight, n))
            neg_g.append(lax.dot_general(weight, s, (((0,), (0,)), ((), ())), preferred_element_type=F32))
        scaled_grad = pos_grad * dst_v + jnp.concatenate(from_neg, axis=0)
        split(g_rel, edges, scaled_grad * src_v)
        split(g_src, edges, scaled_grad * rel_v)
        split(g_dst, edges, pos_grad * scaled)
        split(g_dst, negs, jnp.concatenate(neg_g, axis=0))


def both_terms(h, g):
    both = dot(h, g)
    return both[:, 0:256] + both[:, 256:512]


def reduce_kernel(
    slab,
    index,
    src_rows,
    rel_rows,
    hot_src,
    hot_dst,
    hot_rel,
    embed,
    state,
    new_embed,
    new_state,
    dest_out,
    rel_out,
    g_src,
    g_dst,
    g_rel,
    own_rows,
    own_state,
    rel_far,
    rel_near,
    src_part,
    dst_part,
    rel_pair,
    src_pair,
    dst_pair,
    rel_xy,
    rel_z,
    src_x,
    dst_x,
    src_half,
    src_y,
    dst_y,
    send,
    recv,
    dst_send,
    dst_recv,
    all_recv,
    load_sem,
):
    b, g, z, y, x, c = position()
    sibling = (b, g + 1 - 2 * c)
    opposite = at(z, lax.rem(y + 4, NY), x, c)
    yh = lax.div(y, 4)
    base = lax.rem(b + 3 + NB - x, NB)
    row_of = lax.div(g, 8) * 8 + c
    mine = x * NY + y

    y_order = (4, 3, 5, 2, 6, 1, 7, 0)
    offsets = [(dx, dy) for dx in (2, 1, 3, 0) for dy in y_order if (dx, dy) != (0, 0)]
    z_offsets = (8, 7, 9, 6, 10, 5, 11, 4, 12, 3, 13, 2, 14, 1, 15)

    def plane(dx, dy):
        px, py = lax.rem(x + dx, NX), lax.rem(y + dy, NY)
        return px * NY + py, at(z, py, px, c)

    for dz in z_offsets:
        greet(at(lax.rem(z + dz, NZ), y, x, c))
    for dx, dy in offsets:
        greet(plane(dx, dy)[1])
    for t in range(NX):
        to = (base, row_of + 2 * t)
        source = (lax.rem(b + NB - 3 + t, NB), row_of + 2 * t)

        @pl.when(jnp.logical_or(x != 3, t != 3))
        def _():
            greet(to)
            greet(source)

    greet(sibling)
    load_rows = pltpu.make_async_copy(embed.at[pl.ds(pl.multiple_of(g * 16, 16), 16)], own_rows, load_sem.at[0])
    load_state = pltpu.make_async_copy(state, own_state, load_sem.at[1])
    load_rows.start()
    load_state.start()

    bucket_gradients(index, slab, src_rows, rel_rows, g_src, g_dst, g_rel)
    rel_far[...] = both_terms(hot_rel[pl.ds(1 - c, 1)][0], g_rel[...]).reshape(32, 8, 256)
    pl.semaphore_wait(pltpu.get_barrier_semaphore(), 1 + 15 + 31 + jnp.where(x == 3, 6, 8))

    def pair(source, target, i):
        return remote(source, target, send.at[i], recv.at[i], sibling)

    rel_c = pair(rel_far, rel_pair, 0)
    src_c = pair(src_part.at[:, :, 1 - c], src_pair, 1)
    dst_c = pair(dst_part.at[:, :, 1 - c], dst_pair, 2)
    rel_c.start()
    rel_near[...] = both_terms(hot_rel[pl.ds(c, 1)][0], g_rel[...]).reshape(32, 8, 256)

    rel_c.wait_recv()
    rel_near[...] = rel_near[...] + rel_pair[...]
    for i, (dx, dy) in enumerate(offsets):
        chunk, where = plane(dx, dy)
        remote(rel_near.at[chunk], rel_xy.at[i], send.at[3], recv.at[3], where).start()

    src_part[...] = both_terms(hot_src[...], g_src[...]).reshape(2, 4, 2, 16, 256)
    src_c.start()
    dst_part[...] = both_terms(hot_dst[...], g_dst[...]).reshape(2, 4, 2, 16, 256)
    dst_c.start()
    src_c.wait_recv()
    src_pair[...] = src_pair[...] + src_part[:, :, pl.ds(c, 1)].reshape(2, 4, 16, 256)
    src_sends = []
    for d in (2, 1, 3):
        px = lax.rem(x + d, NX)
        copy = remote(src_pair.at[:, px], src_x.at[d], send.at[4 + d], recv.at[4 + d], at(z, y, px, c))
        copy.start()
        src_sends.append(copy)
    dst_c.wait_recv()
    dst_pair[...] = dst_pair[...] + dst_part[:, :, pl.ds(c, 1)].reshape(2, 4, 16, 256)
    for t in range(NX):
        to = (base, row_of + 2 * t)

        @pl.when(jnp.logical_or(x != 3, t != 3))
        def _():
            remote(dst_pair.at[:, t], dst_x.at[x], dst_send.at[t], dst_recv.at[x], to).start()

    @pl.when(x == 3)
    def _():
        dst_x[3] = dst_pair[:, 3]

    def chunks(ref, n, sem):
        return pltpu.make_async_copy(ref.at[pl.ds(0, n)], ref.at[pl.ds(0, n)], sem)

    chunks(rel_xy, 31, recv.at[3]).wait()
    rel_z[pl.ds(z, 1)] = (rel_near[pl.ds(mine, 1)][0] + jnp.sum(rel_xy[...], axis=0))[None]
    for dz in z_offsets:
        where = at(lax.rem(z + dz, NZ), y, x, c)
        remote(rel_z.at[z], rel_z.at[z], send.at[8], recv.at[8], where).start()

    for copy in src_sends:
        copy.wait_recv()
    src_half[...] = (src_pair[:, pl.ds(x, 1)].reshape(2, 16, 256) + src_x[1]) + (src_x[2] + src_x[3])
    src_far = remote(src_half.at[1 - yh], src_y, send.at[9], recv.at[9], opposite)
    src_far.start()
    for t in range(NX):
        source = (lax.rem(b + NB - 3 + t, NB), row_of + 2 * t)

        @pl.when(jnp.logical_or(x != 3, t != 3))
        def _():
            remote(dst_pair.at[:, t], dst_x.at[t], dst_send.at[t], dst_recv.at[t], source).wait_recv()

    dst_x[0] = (dst_x[0] + dst_x[1]) + (dst_x[2] + dst_x[3])
    dst_far = remote(dst_x.at[0, 1 - yh], dst_y, send.at[10], recv.at[10], opposite)
    dst_far.start()
    load_rows.wait()
    load_state.wait()
    src_far.wait_recv()
    total = src_half[pl.ds(yh, 1)][0] + src_y[...]
    lane = lax.broadcasted_iota(jnp.int32, (16, 256), 1)
    line = lax.broadcasted_iota(jnp.int32, (16, 256), 0)
    old = jnp.sum(jnp.where(lane == line + g * 16, own_state[...], 0.0), axis=1, keepdims=True)
    fresh = old + jnp.sum(total * total, axis=1, keepdims=True) * (1.0 / 256.0)
    new_embed[...] = own_rows[...].astype(F32) - 0.5 * total / jnp.sqrt(fresh)
    lane16 = lax.broadcasted_iota(jnp.int32, (16, 16), 1)
    line16 = lax.broadcasted_iota(jnp.int32, (16, 16), 0)
    new_state[...] = jnp.sum(jnp.where(lane16 == line16, fresh, 0.0), axis=0, keepdims=True)
    dst_far.wait_recv()
    dest_out[...] = dst_x[0, pl.ds(yh, 1)].reshape(16, 256) + dst_y[...]

    chunks(rel_z, 15, recv.at[8]).wait()
    rel_out[pl.ds(c, 1), pl.ds(mine, 1)] = jnp.sum(rel_z[...], axis=0)[None, None]
    for dx, dy in offsets:
        _, where = plane(dx, dy)
        remote(rel_out.at[c, mine], rel_out.at[c, mine], send.at[11], all_recv.at[dx], where).start()
    for dx in (0, 1, 3, 2):
        chunks(rel_xy, 7 if dx == 0 else 8, all_recv.at[dx]).wait()
        group = pl.ds(lax.rem(x + NX - dx, NX) * NY, NY)
        remote(rel_out.at[c, group], rel_out.at[c, group], send.at[12], recv.at[12], sibling).start()
    rel_c.wait_send()
    src_c.wait_send()
    dst_c.wait_send()
    chunks(rel_xy, 31, send.at[3]).wait()
    chunks(rel_z, 15, send.at[8]).wait()
    chunks(rel_xy, 31, send.at[11]).wait()
    for copy in src_sends:
        copy.wait_send()
    for t in range(NX):

        @pl.when(jnp.logical_or(x != 3, t != 3))
        def _():
            remote(dst_pair.at[:, t], dst_x.at[x], dst_send.at[t], dst_recv.at[x], sibling).wait_send()

    src_far.wait_send()
    dst_far.wait_send()
    last = remote(rel_out.at[c], rel_out.at[c], send.at[12], recv.at[12], sibling)
    last.wait_send()
    remote(rel_out.at[1 - c], rel_out.at[1 - c], send.at[12], recv.at[12], sibling).wait_recv()


def finish_kernel(a, b, c, d, a_out, b_out, c_out, d_out, sem):
    copies = [
        pltpu.make_async_copy(held, out, sem.at[i])
        for i, (held, out) in enumerate(((d, d_out), (a, a_out), (c, c_out), (b, b_out)))
    ]
    for copy in copies:
        copy.start()
    for copy in copies:
        copy.wait()


def on_device(embed, state, relation, src_index, dst_index, rel_index, neg_index, counts):
    vmem = pl.BlockSpec(memory_space=pltpu.VMEM)
    hbm = pl.BlockSpec(memory_space=pltpu.HBM)
    dma = pltpu.SemaphoreType.DMA
    i32 = jnp.int32

    def params(**more):
        return pltpu.CompilerParams(vmem_limit_bytes=24 << 20, **more)

    def shape(dims, kind):
        return jax.ShapeDtypeStruct(dims, kind)

    embed, relation, src_index, dst_index, rel_index, neg_index, counts, state = (
        pltpu.with_memory_space_constraint(a, pltpu.HBM)
        for a in (embed, relation, src_index, dst_index, rel_index, neg_index, counts, state.reshape(1, 256))
    )
    passed = pl.pallas_call(
        exchange_kernel,
        out_shape=[
            shape((256, 256), BF16),
            shape((4, 4, 2, 128), i32),
            shape((1024, 256), F32),
            shape((1024, 256), F32),
            shape((256, 1024), BF16),
            shape((256, 2048), BF16),
            shape((2, 256, 1024), BF16),
        ],
        in_specs=[hbm] * 7,
        out_specs=[vmem] * 7,
        scratch_shapes=[
            pltpu.VMEM((256, 256), BF16),
            pltpu.VMEM((512, 256), F32),
            pltpu.VMEM((512, 768), BF16),
            pltpu.VMEM((4, 4, 2, 128), i32),
            pltpu.VMEM((1, 4), i32),
            pltpu.VMEM((4, 4, 2, 128), i32),
            dma((7,)),
            dma((3,)),
            dma((3,)),
            dma((2,)),
            dma((2,)),
        ],
        compiler_params=params(collective_id=0, has_side_effects=True),
        name="exchange",
    )(embed, relation, src_index, dst_index, rel_index, neg_index, counts)
    results = [
        shape((16, 256), F32),
        shape((1, 16), F32),
        shape((16, 256), F32),
        shape((2, 32, 8, 256), F32),
    ]
    found = pl.pallas_call(
        reduce_kernel,
        out_shape=results,
        in_specs=[vmem] * 7 + [hbm] * 2,
        out_specs=[vmem] * 4,
        scratch_shapes=[
            pltpu.VMEM((1024, 512), BF16),
            pltpu.VMEM((2048, 512), BF16),
            pltpu.VMEM((1024, 512), BF16),
            pltpu.VMEM((16, 256), BF16),
            pltpu.VMEM((1, 256), F32),
            pltpu.VMEM((32, 8, 256), F32),
            pltpu.VMEM((32, 8, 256), F32),
            pltpu.VMEM((2, 4, 2, 16, 256), F32),
            pltpu.VMEM((2, 4, 2, 16, 256), F32),
            pltpu.VMEM((32, 8, 256), F32),
            pltpu.VMEM((2, 4, 16, 256), F32),
            pltpu.VMEM((2, 4, 16, 256), F32),
            pltpu.VMEM((31, 8, 256), F32),
            pltpu.VMEM((16, 8, 256), F32),
            pltpu.VMEM((4, 2, 16, 256), F32),
            pltpu.VMEM((4, 2, 16, 256), F32),
            pltpu.VMEM((2, 16, 256), F32),
            pltpu.VMEM((16, 256), F32),
            pltpu.VMEM((16, 256), F32),
            dma((13,)),
            dma((13,)),
            dma((4,)),
            dma((4,)),
            dma((4,)),
            dma((2,)),
        ],
        compiler_params=params(collective_id=1, has_side_effects=True),
        name="reduce",
    )(*passed, embed, state)
    new_embed, new_state, dest, rel_grad = pl.pallas_call(
        finish_kernel,
        out_shape=results,
        in_specs=[vmem] * 4,
        out_specs=[hbm] * 4,
        scratch_shapes=[dma((4,))],
        name="finish",
    )(*found)
    return (new_embed, new_state.reshape(16), dest, rel_grad.reshape(512, 256))


def solution(mesh):
    return jax.shard_map(
        on_device,
        mesh=mesh,
        in_specs=(
            P("blk", None),
            P("blk"),
            P(),
            P("blk", "grp", None, None, None),
            P("blk", "grp", None, None, None),
            P("blk", "grp", None, None, None),
            P("blk", "grp", None, None, None),
            P("blk", "grp", None),
        ),
        out_specs=(P(("blk", "grp"), None), P(("blk", "grp")), P(("blk", "grp"), None), P()),
        check_vma=False,
    )
```

```python
import jax
import jax.numpy as jnp
from jax import lax
from jax.experimental import pallas as pl
from jax.experimental.pallas import tpu as pltpu
from jax.sharding import PartitionSpec as P

NZ = 16
NX = 4
NY = 8
NB = 64
MESH = pl.DeviceIdType.MESH
F32 = jnp.float32
BF16 = jnp.bfloat16


def position():
    b = lax.axis_index("blk")
    g = lax.axis_index("grp")
    z = lax.rem(b, NZ)
    y = lax.div(g, 8) * 4 + lax.div(b, NZ)
    x = lax.rem(lax.div(g, 2), NX)
    c = lax.rem(g, 2)
    return b, g, z, y, x, c


def at(z, y, x, c):
    return (lax.rem(y, 4) * NZ + z, lax.div(y, 4) * 8 + x * 2 + c)


def remote(src, dst, send, recv, where):
    return pltpu.make_async_remote_copy(
        src_ref=src, dst_ref=dst, send_sem=send, recv_sem=recv, device_id=where, device_id_type=MESH
    )


def greet(where):
    pl.semaphore_signal(pltpu.get_barrier_semaphore(), inc=1, device_id=where, device_id_type=MESH)


def dot(a, b):
    return jnp.dot(a, b, preferred_element_type=F32)


def hot(hit):
    return jnp.where(hit, 1.0, 0.0).astype(BF16)


def columns_of(rows):
    turned = rows.T
    return jnp.concatenate([turned[:, 0:1], turned[:, 1:2]], axis=0)


def line_of(rows):
    return jnp.concatenate([rows[0:1], rows[1:2]], axis=1)


def exchange_kernel(
    embed,
    relation,
    src,
    dst,
    rel,
    neg,
    counts,
    slab,
    index,
    src_rows,
    rel_rows,
    hot_src,
    hot_dst,
    hot_rel,
    own,
    table,
    parts,
    loaded,
    live,
    packed,
    load_sem,
    idx_send,
    idx_recv,
    slab_send,
    slab_recv,
):
    b, g, z, y, x, c = position()
    loads = [pltpu.make_async_copy(ref.at[0, 0], loaded.at[i], load_sem.at[i]) for i, ref in enumerate((src, dst, rel, neg))]
    loads.append(pltpu.make_async_copy(counts.at[0], live, load_sem.at[4]))
    load_own = pltpu.make_async_copy(embed, own, load_sem.at[5])
    load_table = pltpu.make_async_copy(relation, table, load_sem.at[6])
    for copy in loads:
        copy.start()
    load_own.start()
    load_table.start()
    sibling = (b, g + 1 - 2 * c)
    ahead = (lax.rem(b + x, NB), g)
    behind = (lax.rem(b + NB - x, NB), g)
    greet(sibling)
    for d in range(1, NX):
        greet(at(z, y, lax.rem(x + d, NX), c))

    @pl.when(x > 0)
    def _():
        greet(behind)

    for copy in loads:
        copy.wait()
    blocks = lax.broadcasted_iota(jnp.int32, (2, 128), 0)
    spots = lax.broadcasted_iota(jnp.int32, (1, 4), 1)
    for t in range(NX):
        count = jnp.sum(jnp.where(spots == t, live[...], 0), axis=1, keepdims=True)
        packed[t, 0] = jnp.where(blocks < count, loaded[0, t], -1)
        for i in range(1, 4):
            packed[t, i] = loaded[i, t]
    load_own.wait()
    pl.semaphore_wait(pltpu.get_barrier_semaphore(), jnp.where(x > 0, NX + 1, NX))

    half = pl.ds(pl.multiple_of(c * 128, 128), 128)
    other = pl.ds(pl.multiple_of((1 - c) * 128, 128), 128)

    @pl.when(x > 0)
    def _():
        remote(own.at[half], slab.at[half], slab_send.at[0], slab_recv.at[0], ahead).start()

    sends = {}
    for d in (2, 1, 3):
        there = lax.rem(x + d, NX)
        sends[d] = remote(packed.at[there], index.at[d], idx_send.at[d - 1], idx_recv.at[d - 1], at(z, y, there, c))
        sends[d].start()
    index[0:1] = packed[pl.ds(x, 1)]

    @pl.when(x == 0)
    def _():
        slab[...] = own[...]

    load_table.wait()
    r = table[...]
    high = r.astype(BF16)
    rest = r - high.astype(F32)
    middle = rest.astype(BF16)
    parts[:, 0:256] = high
    parts[:, 256:512] = middle
    parts[:, 512:768] = (rest - middle.astype(F32)).astype(BF16)
    lane = lax.broadcasted_iota(jnp.int32, (256, 256), 1)
    lane_r = lax.broadcasted_iota(jnp.int32, (256, 512), 1)
    sub = lax.broadcasted_iota(jnp.int32, (256, 256), 0)
    sub_r = lax.broadcasted_iota(jnp.int32, (2, 256, 256), 0) * 256 + lax.broadcasted_iota(jnp.int32, (2, 256, 256), 1)
    for k, d in enumerate((0, 1, 3, 2)):
        edges = slice(k * 256, k * 256 + 256)
        negs = slice(1024 + k * 256, 1024 + k * 256 + 256)
        if d > 0:
            sends[d].wait_recv()
        src_rows[edges] = dot(hot(lane == columns_of(index[d, 0])), own[...])
        pieces = dot(hot(lane_r == columns_of(index[d, 2])), parts[...])
        rel_rows[edges] = (pieces[:, 0:256] + pieces[:, 256:512]) + pieces[:, 512:768]
        hot_src[:, edges] = hot(sub == line_of(index[d, 0]))
        hot_dst[:, edges] = hot(sub == line_of(index[d, 1]))
        hot_dst[:, negs] = hot(sub == line_of(index[d, 3]))
        hot_rel[:, :, edges] = hot(sub_r == line_of(index[d, 2])[None])

    @pl.when(x > 0)
    def _():
        first = remote(own.at[half], slab.at[half], slab_send.at[0], slab_recv.at[0], ahead)
        second = remote(slab.at[half], slab.at[half], slab_send.at[1], slab_recv.at[1], sibling)
        first.wait_recv()
        second.start()
        first.wait_send()
        second.wait_send()
        remote(slab.at[other], slab.at[other], slab_send.at[1], slab_recv.at[1], sibling).wait_recv()

    for d in (1, 2, 3):
        sends[d].wait_send()


def bucket_gradients(index, slab, src_rows, rel_rows, g_src, g_dst, g_rel):
    def split(ref, rows, value):
        top = value.astype(BF16)
        ref[rows, 0:256] = top
        ref[rows, 256:512] = (value - top.astype(F32)).astype(BF16)

    lane = lax.broadcasted_iota(jnp.int32, (256, 256), 1)
    for k, d in enumerate((0, 1, 3, 2)):
        edges = slice(k * 256, k * 256 + 256)
        negs = slice(1024 + k * 256, 1024 + k * 256 + 256)
        src_v = src_rows[edges]
        rel_v = rel_rows[edges]
        dst_v = dot(hot(lane == columns_of(index[d, 1])), slab[...])
        neg_v = dot(hot(lane == columns_of(index[d, 3])), slab[...]).astype(BF16)
        scaled = src_v * rel_v
        positive = jnp.sum(scaled * dst_v, axis=1, keepdims=True)
        pos_grad = -jax.nn.sigmoid(-positive)
        scaled_b = scaled.astype(BF16)
        from_neg = []
        neg_g = []
        for j in range(2):
            block = slice(j * 128, j * 128 + 128)
            s, n = scaled_b[block], neg_v[block]
            score = lax.dot_general(s, n, (((1,), (1,)), ((), ())), preferred_element_type=F32)
            weight = (jax.nn.sigmoid(score) * (1.0 / 128.0)).astype(BF16)
            from_neg.append(dot(weight, n))
            neg_g.append(lax.dot_general(weight, s, (((0,), (0,)), ((), ())), preferred_element_type=F32))
        scaled_grad = pos_grad * dst_v + jnp.concatenate(from_neg, axis=0)
        split(g_rel, edges, scaled_grad * src_v)
        split(g_src, edges, scaled_grad * rel_v)
        split(g_dst, edges, pos_grad * scaled)
        split(g_dst, negs, jnp.concatenate(neg_g, axis=0))


def both_terms(h, g):
    both = dot(h, g)
    return both[:, 0:256] + both[:, 256:512]


def reduce_kernel(
    slab,
    index,
    src_rows,
    rel_rows,
    hot_src,
    hot_dst,
    hot_rel,
    embed,
    state,
    new_embed,
    new_state,
    dest_out,
    rel_out,
    g_src,
    g_dst,
    g_rel,
    own_rows,
    own_state,
    rel_far,
    rel_near,
    src_part,
    dst_part,
    rel_pair,
    src_pair,
    dst_pair,
    rel_xy,
    rel_z,
    src_x,
    dst_x,
    src_half,
    src_y,
    dst_y,
    send,
    recv,
    dst_send,
    dst_recv,
    all_recv,
    load_sem,
):
    b, g, z, y, x, c = position()
    sibling = (b, g + 1 - 2 * c)
    opposite = at(z, lax.rem(y + 4, NY), x, c)
    yh = lax.div(y, 4)
    base = lax.rem(b + 3 + NB - x, NB)
    row_of = lax.div(g, 8) * 8 + c
    mine = x * NY + y

    y_order = (4, 3, 5, 2, 6, 1, 7, 0)
    offsets = [(dx, dy) for dx in (2, 1, 3, 0) for dy in y_order if (dx, dy) != (0, 0)]
    z_offsets = (8, 7, 9, 6, 10, 5, 11, 4, 12, 3, 13, 2, 14, 1, 15)

    def plane(dx, dy):
        px, py = lax.rem(x + dx, NX), lax.rem(y + dy, NY)
        return px * NY + py, at(z, py, px, c)

    for dz in z_offsets:
        greet(at(lax.rem(z + dz, NZ), y, x, c))
    for dx, dy in offsets:
        greet(plane(dx, dy)[1])
    for t in range(NX):
        source = (lax.rem(b + NB - 3 + t, NB), row_of + 2 * t)

        @pl.when(jnp.logical_or(x != 3, t != 3))
        def _():
            greet(source)

    greet(sibling)
    load_rows = pltpu.make_async_copy(embed.at[pl.ds(pl.multiple_of(g * 16, 16), 16)], own_rows, load_sem.at[0])
    load_state = pltpu.make_async_copy(state, own_state, load_sem.at[1])
    load_rows.start()
    load_state.start()

    bucket_gradients(index, slab, src_rows, rel_rows, g_src, g_dst, g_rel)
    rel_far[...] = both_terms(hot_rel[pl.ds(1 - c, 1)][0], g_rel[...]).reshape(32, 8, 256)
    pl.semaphore_wait(pltpu.get_barrier_semaphore(), 1 + 15 + 31 + jnp.where(x == 3, 3, 4))

    def pair(source, target, i):
        return remote(source, target, send.at[i], recv.at[i], sibling)

    rel_c = pair(rel_far, rel_pair, 0)
    src_c = pair(src_part.at[:, :, 1 - c], src_pair, 1)
    dst_c = pair(dst_part.at[:, :, 1 - c], dst_pair, 2)
    rel_c.start()
    rel_near[...] = both_terms(hot_rel[pl.ds(c, 1)][0], g_rel[...]).reshape(32, 8, 256)

    rel_c.wait_recv()
    rel_near[...] = rel_near[...] + rel_pair[...]
    for i, (dx, dy) in enumerate(offsets):
        chunk, where = plane(dx, dy)
        remote(rel_near.at[chunk], rel_xy.at[i], send.at[3], recv.at[3], where).start()

    dst_part[...] = both_terms(hot_dst[...], g_dst[...]).reshape(2, 4, 2, 16, 256)
    dst_c.start()
    src_part[...] = both_terms(hot_src[...], g_src[...]).reshape(2, 4, 2, 16, 256)
    dst_c.wait_recv()
    dst_pair[...] = dst_pair[...] + dst_part[:, :, pl.ds(c, 1)].reshape(2, 4, 16, 256)
    for t in range(NX):
        to = (base, row_of + 2 * t)

        @pl.when(jnp.logical_or(x != 3, t != 3))
        def _():
            remote(dst_pair.at[:, t], dst_x.at[x], dst_send.at[t], dst_recv.at[x], to).start()

    @pl.when(x == 3)
    def _():
        dst_x[3] = dst_pair[:, 3]

    src_c.start()

    def chunks(ref, n, sem):
        return pltpu.make_async_copy(ref.at[pl.ds(0, n)], ref.at[pl.ds(0, n)], sem)

    chunks(rel_xy, 31, recv.at[3]).wait()
    rel_z[pl.ds(z, 1)] = (rel_near[pl.ds(mine, 1)][0] + jnp.sum(rel_xy[...], axis=0))[None]
    for dz in z_offsets:
        where = at(lax.rem(z + dz, NZ), y, x, c)
        remote(rel_z.at[z], rel_z.at[z], send.at[8], recv.at[8], where).start()

    src_c.wait_recv()
    src_pair[...] = src_pair[...] + src_part[:, :, pl.ds(c, 1)].reshape(2, 4, 16, 256)
    src_sends = []
    for d in (2, 1, 3):
        px = lax.rem(x + d, NX)
        copy = remote(src_pair.at[:, px], src_x.at[d], send.at[4 + d], recv.at[4 + d], at(z, y, px, c))
        copy.start()
        src_sends.append(copy)
    for copy in src_sends:
        copy.wait_recv()
    src_half[...] = (src_pair[:, pl.ds(x, 1)].reshape(2, 16, 256) + src_x[1]) + (src_x[2] + src_x[3])
    src_far = remote(src_half.at[1 - yh], src_y, send.at[9], recv.at[9], opposite)
    src_far.start()
    for t in range(NX):
        source = (lax.rem(b + NB - 3 + t, NB), row_of + 2 * t)

        @pl.when(jnp.logical_or(x != 3, t != 3))
        def _():
            remote(dst_pair.at[:, t], dst_x.at[t], dst_send.at[t], dst_recv.at[t], source).wait_recv()

    dst_x[0] = (dst_x[0] + dst_x[1]) + (dst_x[2] + dst_x[3])
    dst_far = remote(dst_x.at[0, 1 - yh], dst_y, send.at[10], recv.at[10], opposite)
    dst_far.start()
    chunks(rel_z, 15, recv.at[8]).wait()
    rel_out[pl.ds(c, 1), pl.ds(mine, 1)] = jnp.sum(rel_z[...], axis=0)[None, None]
    for dx, dy in offsets:
        _, where = plane(dx, dy)
        remote(rel_out.at[c, mine], rel_out.at[c, mine], send.at[11], all_recv.at[dx], where).start()
    load_rows.wait()
    load_state.wait()
    src_far.wait_recv()
    total = src_half[pl.ds(yh, 1)][0] + src_y[...]
    lane = lax.broadcasted_iota(jnp.int32, (16, 256), 1)
    line = lax.broadcasted_iota(jnp.int32, (16, 256), 0)
    old = jnp.sum(jnp.where(lane == line + g * 16, own_state[...], 0.0), axis=1, keepdims=True)
    fresh = old + jnp.sum(total * total, axis=1, keepdims=True) * (1.0 / 256.0)
    new_embed[...] = own_rows[...].astype(F32) - 0.5 * total / jnp.sqrt(fresh)
    lane16 = lax.broadcasted_iota(jnp.int32, (16, 16), 1)
    line16 = lax.broadcasted_iota(jnp.int32, (16, 16), 0)
    new_state[...] = jnp.sum(jnp.where(lane16 == line16, fresh, 0.0), axis=0, keepdims=True)
    for dx in (0, 1, 3, 2):
        chunks(rel_xy, 7 if dx == 0 else 8, all_recv.at[dx]).wait()
        group = pl.ds(lax.rem(x + NX - dx, NX) * NY, NY)
        remote(rel_out.at[c, group], rel_out.at[c, group], send.at[12], recv.at[12], sibling).start()
    dst_far.wait_recv()
    dest_out[...] = dst_x[0, pl.ds(yh, 1)].reshape(16, 256) + dst_y[...]
    rel_c.wait_send()
    src_c.wait_send()
    dst_c.wait_send()
    chunks(rel_xy, 31, send.at[3]).wait()
    chunks(rel_z, 15, send.at[8]).wait()
    chunks(rel_xy, 31, send.at[11]).wait()
    for copy in src_sends:
        copy.wait_send()
    for t in range(NX):

        @pl.when(jnp.logical_or(x != 3, t != 3))
        def _():
            remote(dst_pair.at[:, t], dst_x.at[x], dst_send.at[t], dst_recv.at[x], sibling).wait_send()

    src_far.wait_send()
    dst_far.wait_send()
    last = remote(rel_out.at[c], rel_out.at[c], send.at[12], recv.at[12], sibling)
    last.wait_send()
    remote(rel_out.at[1 - c], rel_out.at[1 - c], send.at[12], recv.at[12], sibling).wait_recv()


def finish_kernel(a, b, c, d, a_out, b_out, c_out, d_out, sem):
    copies = [
        pltpu.make_async_copy(held, out, sem.at[i])
        for i, (held, out) in enumerate(((d, d_out), (a, a_out), (c, c_out), (b, b_out)))
    ]
    for copy in copies:
        copy.start()
    for copy in copies:
        copy.wait()


def on_device(embed, state, relation, src_index, dst_index, rel_index, neg_index, counts):
    vmem = pl.BlockSpec(memory_space=pltpu.VMEM)
    hbm = pl.BlockSpec(memory_space=pltpu.HBM)
    dma = pltpu.SemaphoreType.DMA
    i32 = jnp.int32

    def params(**more):
        return pltpu.CompilerParams(vmem_limit_bytes=24 << 20, **more)

    def shape(dims, kind):
        return jax.ShapeDtypeStruct(dims, kind)

    embed, relation, src_index, dst_index, rel_index, neg_index, counts, state = (
        pltpu.with_memory_space_constraint(a, pltpu.HBM)
        for a in (embed, relation, src_index, dst_index, rel_index, neg_index, counts, state.reshape(1, 256))
    )
    passed = pl.pallas_call(
        exchange_kernel,
        out_shape=[
            shape((256, 256), BF16),
            shape((4, 4, 2, 128), i32),
            shape((1024, 256), F32),
            shape((1024, 256), F32),
            shape((256, 1024), BF16),
            shape((256, 2048), BF16),
            shape((2, 256, 1024), BF16),
        ],
        in_specs=[hbm] * 7,
        out_specs=[vmem] * 7,
        scratch_shapes=[
            pltpu.VMEM((256, 256), BF16),
            pltpu.VMEM((512, 256), F32),
            pltpu.VMEM((512, 768), BF16),
            pltpu.VMEM((4, 4, 2, 128), i32),
            pltpu.VMEM((1, 4), i32),
            pltpu.VMEM((4, 4, 2, 128), i32),
            dma((7,)),
            dma((3,)),
            dma((3,)),
            dma((2,)),
            dma((2,)),
        ],
        compiler_params=params(collective_id=0, has_side_effects=True),
        name="exchange",
    )(embed, relation, src_index, dst_index, rel_index, neg_index, counts)
    results = [
        shape((16, 256), F32),
        shape((1, 16), F32),
        shape((16, 256), F32),
        shape((2, 32, 8, 256), F32),
    ]
    found = pl.pallas_call(
        reduce_kernel,
        out_shape=results,
        in_specs=[vmem] * 7 + [hbm] * 2,
        out_specs=[vmem] * 4,
        scratch_shapes=[
            pltpu.VMEM((1024, 512), BF16),
            pltpu.VMEM((2048, 512), BF16),
            pltpu.VMEM((1024, 512), BF16),
            pltpu.VMEM((16, 256), BF16),
            pltpu.VMEM((1, 256), F32),
            pltpu.VMEM((32, 8, 256), F32),
            pltpu.VMEM((32, 8, 256), F32),
            pltpu.VMEM((2, 4, 2, 16, 256), F32),
            pltpu.VMEM((2, 4, 2, 16, 256), F32),
            pltpu.VMEM((32, 8, 256), F32),
            pltpu.VMEM((2, 4, 16, 256), F32),
            pltpu.VMEM((2, 4, 16, 256), F32),
            pltpu.VMEM((31, 8, 256), F32),
            pltpu.VMEM((16, 8, 256), F32),
            pltpu.VMEM((4, 2, 16, 256), F32),
            pltpu.VMEM((4, 2, 16, 256), F32),
            pltpu.VMEM((2, 16, 256), F32),
            pltpu.VMEM((16, 256), F32),
            pltpu.VMEM((16, 256), F32),
            dma((13,)),
            dma((13,)),
            dma((4,)),
            dma((4,)),
            dma((4,)),
            dma((2,)),
        ],
        compiler_params=params(collective_id=1, has_side_effects=True),
        name="reduce",
    )(*passed, embed, state)
    new_embed, new_state, dest, rel_grad = pl.pallas_call(
        finish_kernel,
        out_shape=results,
        in_specs=[vmem] * 4,
        out_specs=[hbm] * 4,
        scratch_shapes=[dma((4,))],
        compiler_params=pltpu.CompilerParams(vmem_limit_bytes=4 << 20),
        name="finish",
    )(*found)
    return (new_embed, new_state.reshape(16), dest, rel_grad.reshape(512, 256))


def solution(mesh):
    return jax.shard_map(
        on_device,
        mesh=mesh,
        in_specs=(
            P("blk", None),
            P("blk"),
            P(),
            P("blk", "grp", None, None, None),
            P("blk", "grp", None, None, None),
            P("blk", "grp", None, None, None),
            P("blk", "grp", None, None, None),
            P("blk", "grp", None),
        ),
        out_specs=(P(("blk", "grp"), None), P(("blk", "grp")), P(("blk", "grp"), None), P()),
        check_vma=False,
    )
```

```python
import jax
import jax.numpy as jnp
from jax import lax
from jax.experimental import pallas as pl
from jax.experimental.pallas import tpu as pltpu
from jax.sharding import PartitionSpec as P

NZ = 16
NX = 4
NY = 8
NB = 64
MESH = pl.DeviceIdType.MESH
F32 = jnp.float32
BF16 = jnp.bfloat16


def position():
    b = lax.axis_index("blk")
    g = lax.axis_index("grp")
    z = lax.rem(b, NZ)
    y = lax.div(g, 8) * 4 + lax.div(b, NZ)
    x = lax.rem(lax.div(g, 2), NX)
    c = lax.rem(g, 2)
    return b, g, z, y, x, c


def at(z, y, x, c):
    return (lax.rem(y, 4) * NZ + z, lax.div(y, 4) * 8 + x * 2 + c)


def remote(src, dst, send, recv, where):
    return pltpu.make_async_remote_copy(
        src_ref=src, dst_ref=dst, send_sem=send, recv_sem=recv, device_id=where, device_id_type=MESH
    )


def greet(where):
    pl.semaphore_signal(pltpu.get_barrier_semaphore(), inc=1, device_id=where, device_id_type=MESH)


def dot(a, b):
    return jnp.dot(a, b, preferred_element_type=F32)


def hot(hit):
    return jnp.where(hit, 1.0, 0.0).astype(BF16)


def columns_of(rows):
    turned = rows.T
    return jnp.concatenate([turned[:, 0:1], turned[:, 1:2]], axis=0)


def line_of(rows):
    return jnp.concatenate([rows[0:1], rows[1:2]], axis=1)


def bucket_gradients(index, slab, src_rows, rel_rows, g_src, g_dst, g_rel):
    def split(ref, rows, value):
        top = value.astype(BF16)
        ref[rows, 0:256] = top
        ref[rows, 256:512] = (value - top.astype(F32)).astype(BF16)

    lane = lax.broadcasted_iota(jnp.int32, (256, 256), 1)
    for k, d in enumerate((0, 1, 3, 2)):
        edges = slice(k * 256, k * 256 + 256)
        negs = slice(1024 + k * 256, 1024 + k * 256 + 256)
        src_v = src_rows[edges]
        rel_v = rel_rows[edges]
        dst_v = dot(hot(lane == columns_of(index[d, 1])), slab[...])
        neg_v = dot(hot(lane == columns_of(index[d, 3])), slab[...]).astype(BF16)
        scaled = src_v * rel_v
        positive = jnp.sum(scaled * dst_v, axis=1, keepdims=True)
        pos_grad = -jax.nn.sigmoid(-positive)
        scaled_b = scaled.astype(BF16)
        from_neg = []
        neg_g = []
        for j in range(2):
            block = slice(j * 128, j * 128 + 128)
            s, n = scaled_b[block], neg_v[block]
            score = lax.dot_general(s, n, (((1,), (1,)), ((), ())), preferred_element_type=F32)
            weight = (jax.nn.sigmoid(score) * (1.0 / 128.0)).astype(BF16)
            from_neg.append(dot(weight, n))
            neg_g.append(lax.dot_general(weight, s, (((0,), (0,)), ((), ())), preferred_element_type=F32))
        scaled_grad = pos_grad * dst_v + jnp.concatenate(from_neg, axis=0)
        split(g_rel, edges, scaled_grad * src_v)
        split(g_src, edges, scaled_grad * rel_v)
        split(g_dst, edges, pos_grad * scaled)
        split(g_dst, negs, jnp.concatenate(neg_g, axis=0))


def both_terms(h, g):
    both = dot(h, g)
    return both[:, 0:256] + both[:, 256:512]


def window_kernel(
    embed,
    relation,
    src,
    dst,
    rel,
    neg,
    counts,
    state,
    new_embed,
    new_state,
    dest_out,
    rel_out,
    slab,
    index,
    src_rows,
    rel_rows,
    hot_src,
    hot_dst,
    hot_rel,
    own,
    table,
    parts,
    loaded,
    live,
    packed,
    g_src,
    g_dst,
    g_rel,
    own_state,
    rel_far,
    rel_near,
    src_part,
    dst_part,
    rel_pair,
    src_pair,
    dst_pair,
    rel_xy,
    rel_z,
    src_x,
    dst_x,
    src_half,
    src_y,
    dst_y,
    load_sem,
    idx_send,
    idx_recv,
    slab_send,
    slab_recv,
    send,
    recv,
    dst_send,
    dst_recv,
    pair_recv,
    all_recv,
    here,
):
    b, g, z, y, x, c = position()
    loads = [pltpu.make_async_copy(ref.at[0, 0], loaded.at[i], load_sem.at[i]) for i, ref in enumerate((src, dst, rel, neg))]
    loads.append(pltpu.make_async_copy(counts.at[0], live, load_sem.at[4]))
    load_own = pltpu.make_async_copy(embed, own, load_sem.at[5])
    load_table = pltpu.make_async_copy(relation, table, load_sem.at[6])
    load_state = pltpu.make_async_copy(state, own_state, load_sem.at[7])
    for copy in loads:
        copy.start()
    load_own.start()
    load_table.start()
    load_state.start()

    sibling = (b, g + 1 - 2 * c)
    ahead = (lax.rem(b + x, NB), g)
    behind = (lax.rem(b + NB - x, NB), g)
    opposite = at(z, lax.rem(y + 4, NY), x, c)
    yh = lax.div(y, 4)
    base = lax.rem(b + 3 + NB - x, NB)
    row_of = lax.div(g, 8) * 8 + c
    mine = x * NY + y

    y_order = (4, 3, 5, 2, 6, 1, 7, 0)
    z_offsets = (8, 7, 9, 6, 10, 5, 11, 4, 12, 3, 13, 2, 14, 1, 15)

    def plane(dx, dy):
        px, py = lax.rem(x + dx, NX), lax.rem(y + dy, NY)
        return px * NY + py, at(z, py, px, c)

    def along_x(d):
        return at(z, y, lax.rem(x + d, NX), c)

    def along_y(d):
        return at(z, lax.rem(y + NY + d, NY), x, c)

    def along_z(d):
        return at(lax.rem(z + NZ + d, NZ), y, x, c)

    def tell(i, *wheres):
        for where in wheres:
            pl.semaphore_signal(here.at[i], inc=1, device_id=where, device_id_type=MESH)

    greet(sibling)
    for d in (2, 1, 3):
        greet(along_x(d))
    for d in (1, -1):
        greet(along_y(d))
        greet(along_z(d))

    @pl.when(x > 0)
    def _():
        greet(behind)

    for copy in loads:
        copy.wait()
    blocks = lax.broadcasted_iota(jnp.int32, (2, 128), 0)
    spots = lax.broadcasted_iota(jnp.int32, (1, 4), 1)
    for t in range(NX):
        count = jnp.sum(jnp.where(spots == t, live[...], 0), axis=1, keepdims=True)
        packed[t, 0] = jnp.where(blocks < count, loaded[0, t], -1)
        for i in range(1, 4):
            packed[t, i] = loaded[i, t]
    load_own.wait()
    pl.semaphore_wait(pltpu.get_barrier_semaphore(), jnp.where(x > 0, 9, 8))

    half = pl.ds(pl.multiple_of(c * 128, 128), 128)
    other = pl.ds(pl.multiple_of((1 - c) * 128, 128), 128)

    @pl.when(x > 0)
    def _():
        remote(own.at[half], slab.at[half], slab_send.at[0], slab_recv.at[0], ahead).start()

    sends = {}
    for d in (2, 1, 3):
        there = lax.rem(x + d, NX)
        sends[d] = remote(packed.at[there], index.at[d], idx_send.at[d - 1], idx_recv.at[d - 1], along_x(d))
        sends[d].start()
    tell(0, along_y(1), along_y(-1))
    tell(1, along_z(1), along_z(-1))
    index[0:1] = packed[pl.ds(x, 1)]

    @pl.when(x == 0)
    def _():
        slab[...] = own[...]

    load_table.wait()
    r = table[...]
    high = r.astype(BF16)
    rest = r - high.astype(F32)
    middle = rest.astype(BF16)
    parts[:, 0:256] = high
    parts[:, 256:512] = middle
    parts[:, 512:768] = (rest - middle.astype(F32)).astype(BF16)

    lane = lax.broadcasted_iota(jnp.int32, (256, 256), 1)
    lane_r = lax.broadcasted_iota(jnp.int32, (256, 512), 1)
    sub = lax.broadcasted_iota(jnp.int32, (256, 256), 0)
    sub_r = lax.broadcasted_iota(jnp.int32, (2, 256, 256), 0) * 256 + lax.broadcasted_iota(jnp.int32, (2, 256, 256), 1)
    for k, d in enumerate((0, 1, 3, 2)):
        edges = slice(k * 256, k * 256 + 256)
        negs = slice(1024 + k * 256, 1024 + k * 256 + 256)
        if k == 1:
            pl.semaphore_wait(here.at[0], 2)
            pl.semaphore_wait(here.at[1], 2)
            tell(2, along_y(2), along_y(-2))
            tell(3, along_z(2), along_z(-2))
        if k == 2:
            pl.semaphore_wait(here.at[2], 2)
            pl.semaphore_wait(here.at[3], 2)
            tell(4, along_x(2), along_x(1), along_x(3))
            tell(5, along_z(4), along_z(-4))
        if k == 3:
            pl.semaphore_wait(here.at[4], 3)

            @pl.when(x < 3)
            def _():
                tell(6, along_z(x - 3))

        if d > 0:
            sends[d].wait_recv()
        src_rows[edges] = dot(hot(lane == columns_of(index[d, 0])), own[...])
        pieces = dot(hot(lane_r == columns_of(index[d, 2])), parts[...])
        rel_rows[edges] = (pieces[:, 0:256] + pieces[:, 256:512]) + pieces[:, 512:768]
        hot_src[:, edges] = hot(sub == line_of(index[d, 0]))
        hot_dst[:, edges] = hot(sub == line_of(index[d, 1]))
        hot_dst[:, negs] = hot(sub == line_of(index[d, 3]))
        hot_rel[:, :, edges] = hot(sub_r == line_of(index[d, 2])[None])

    @pl.when(x > 0)
    def _():
        first = remote(own.at[half], slab.at[half], slab_send.at[0], slab_recv.at[0], ahead)
        second = remote(slab.at[half], slab.at[half], slab_send.at[1], slab_recv.at[1], sibling)
        first.wait_recv()
        second.start()
        first.wait_send()
        second.wait_send()
        remote(slab.at[other], slab.at[other], slab_send.at[1], slab_recv.at[1], sibling).wait_recv()

    for d in (1, 2, 3):
        sends[d].wait_send()

    bucket_gradients(index, slab, src_rows, rel_rows, g_src, g_dst, g_rel)
    rel_far[...] = both_terms(hot_rel[pl.ds(1 - c, 1)][0], g_rel[...]).reshape(32, 8, 256)

    def pair(source, target, i):
        return remote(source, target, send.at[i], recv.at[i], sibling)

    src_c = pair(src_part.at[:, :, 1 - c], src_pair, 1)
    dst_c = pair(dst_part.at[:, :, 1 - c], dst_pair, 2)

    rel_c = {}
    for dx in (2, 1, 3, 0):
        rows = pl.ds(lax.rem(x + dx, NX) * NY, NY)
        mirror = pl.ds(lax.rem(x + dx, NX) * NY, NY)
        rel_c[dx] = remote(rel_far.at[rows], rel_pair.at[mirror], send.at[0], pair_recv.at[dx], sibling)
        rel_c[dx].start()
    rel_near[...] = both_terms(hot_rel[pl.ds(c, 1)][0], g_rel[...]).reshape(32, 8, 256)
    for dx in (2, 1, 3, 0):
        rows = pl.ds(lax.rem(x + dx, NX) * NY, NY)
        rel_c[dx].wait_recv()
        rel_near[rows] = rel_near[rows] + rel_pair[rows]
        for dy in y_order:
            if (dx, dy) != (0, 0):
                chunk, where = plane(dx, dy)
                remote(rel_near.at[chunk], rel_xy.at[(dx * NY + dy) - 1], send.at[3], recv.at[3], where).start()

    dst_part[...] = both_terms(hot_dst[...], g_dst[...]).reshape(2, 4, 2, 16, 256)
    dst_c.start()
    src_part[...] = both_terms(hot_src[...], g_src[...]).reshape(2, 4, 2, 16, 256)
    dst_c.wait_recv()
    dst_pair[...] = dst_pair[...] + dst_part[:, :, pl.ds(c, 1)].reshape(2, 4, 16, 256)
    @pl.when(x < 3)
    def _():
        pl.semaphore_wait(here.at[6], 1)

    for t in range(NX):
        to = (base, row_of + 2 * t)

        @pl.when(jnp.logical_or(x != 3, t != 3))
        def _():
            remote(dst_pair.at[:, t], dst_x.at[x], dst_send.at[t], dst_recv.at[x], to).start()

    @pl.when(x == 3)
    def _():
        dst_x[3] = dst_pair[:, 3]

    src_c.start()

    offsets = [(dx, dy) for dx in (2, 1, 3, 0) for dy in y_order if (dx, dy) != (0, 0)]

    def chunks(ref, n, sem):
        return pltpu.make_async_copy(ref.at[pl.ds(0, n)], ref.at[pl.ds(0, n)], sem)

    chunks(rel_xy, 31, recv.at[3]).wait()
    rel_z[pl.ds(z, 1)] = (rel_near[pl.ds(mine, 1)][0] + jnp.sum(rel_xy[...], axis=0))[None]
    pl.semaphore_wait(here.at[5], 2)
    for dz in z_offsets:
        where = along_z(dz)
        remote(rel_z.at[z], rel_z.at[z], send.at[8], recv.at[8], where).start()

    src_c.wait_recv()
    src_pair[...] = src_pair[...] + src_part[:, :, pl.ds(c, 1)].reshape(2, 4, 16, 256)
    src_sends = []
    for d in (2, 1, 3):
        px = lax.rem(x + d, NX)
        copy = remote(src_pair.at[:, px], src_x.at[d], send.at[4 + d], recv.at[4 + d], at(z, y, px, c))
        copy.start()
        src_sends.append(copy)
    for copy in src_sends:
        copy.wait_recv()
    src_half[...] = (src_pair[:, pl.ds(x, 1)].reshape(2, 16, 256) + src_x[1]) + (src_x[2] + src_x[3])
    src_far = remote(src_half.at[1 - yh], src_y, send.at[9], recv.at[9], opposite)
    src_far.start()
    for t in range(NX):
        source = (lax.rem(b + NB - 3 + t, NB), row_of + 2 * t)

        @pl.when(jnp.logical_or(x != 3, t != 3))
        def _():
            remote(dst_pair.at[:, t], dst_x.at[t], dst_send.at[t], dst_recv.at[t], source).wait_recv()

    dst_x[0] = (dst_x[0] + dst_x[1]) + (dst_x[2] + dst_x[3])
    dst_far = remote(dst_x.at[0, 1 - yh], dst_y, send.at[10], recv.at[10], opposite)
    dst_far.start()
    chunks(rel_z, 15, recv.at[8]).wait()
    rel_out[pl.ds(c, 1), pl.ds(mine, 1)] = jnp.sum(rel_z[...], axis=0)[None, None]
    for dx, dy in offsets:
        _, where = plane(dx, dy)
        remote(rel_out.at[c, mine], rel_out.at[c, mine], send.at[11], all_recv.at[dx], where).start()
    load_state.wait()
    src_far.wait_recv()
    total = src_half[pl.ds(yh, 1)][0] + src_y[...]
    lane = lax.broadcasted_iota(jnp.int32, (16, 256), 1)
    line = lax.broadcasted_iota(jnp.int32, (16, 256), 0)
    old = jnp.sum(jnp.where(lane == line + g * 16, own_state[...], 0.0), axis=1, keepdims=True)
    fresh = old + jnp.sum(total * total, axis=1, keepdims=True) * (1.0 / 256.0)
    new_embed[...] = own[pl.ds(pl.multiple_of(g * 16, 16), 16)].astype(F32) - 0.5 * total / jnp.sqrt(fresh)
    lane16 = lax.broadcasted_iota(jnp.int32, (16, 16), 1)
    line16 = lax.broadcasted_iota(jnp.int32, (16, 16), 0)
    new_state[...] = jnp.sum(jnp.where(lane16 == line16, fresh, 0.0), axis=0, keepdims=True)
    for dx in (0, 1, 3, 2):
        chunks(rel_xy, 7 if dx == 0 else 8, all_recv.at[dx]).wait()
        group = pl.ds(lax.rem(x + NX - dx, NX) * NY, NY)
        remote(rel_out.at[c, group], rel_out.at[c, group], send.at[12], recv.at[12], sibling).start()
    dst_far.wait_recv()
    dest_out[...] = dst_x[0, pl.ds(yh, 1)].reshape(16, 256) + dst_y[...]
    remote(rel_far, rel_pair, send.at[0], recv.at[0], sibling).wait_send()
    src_c.wait_send()
    dst_c.wait_send()
    chunks(rel_xy, 31, send.at[3]).wait()
    chunks(rel_z, 15, send.at[8]).wait()
    chunks(rel_xy, 31, send.at[11]).wait()
    for copy in src_sends:
        copy.wait_send()
    for t in range(NX):

        @pl.when(jnp.logical_or(x != 3, t != 3))
        def _():
            remote(dst_pair.at[:, t], dst_x.at[x], dst_send.at[t], dst_recv.at[x], sibling).wait_send()

    src_far.wait_send()
    dst_far.wait_send()
    last = remote(rel_out.at[c], rel_out.at[c], send.at[12], recv.at[12], sibling)
    last.wait_send()
    remote(rel_out.at[1 - c], rel_out.at[1 - c], send.at[12], recv.at[12], sibling).wait_recv()


def finish_kernel(a, b, c, d, a_out, b_out, c_out, d_out, sem):
    copies = [
        pltpu.make_async_copy(held, out, sem.at[i])
        for i, (held, out) in enumerate(((d, d_out), (a, a_out), (c, c_out), (b, b_out)))
    ]
    for copy in copies:
        copy.start()
    for copy in copies:
        copy.wait()


def on_device(embed, state, relation, src_index, dst_index, rel_index, neg_index, counts):
    vmem = pl.BlockSpec(memory_space=pltpu.VMEM)
    hbm = pl.BlockSpec(memory_space=pltpu.HBM)
    dma = pltpu.SemaphoreType.DMA

    def held(dims, kind=F32):
        return pltpu.VMEM(dims, kind)

    results = [
        jax.ShapeDtypeStruct(dims, F32) for dims in ((16, 256), (1, 16), (16, 256), (2, 32, 8, 256))
    ]
    given = (embed, relation, src_index, dst_index, rel_index, neg_index, counts, state.reshape(1, 256))
    found = pl.pallas_call(
        window_kernel,
        out_shape=results,
        in_specs=[hbm] * 8,
        out_specs=[vmem] * 4,
        scratch_shapes=[
            held((256, 256), BF16),
            held((4, 4, 2, 128), jnp.int32),
            held((1024, 256)),
            held((1024, 256)),
            held((256, 1024), BF16),
            held((256, 2048), BF16),
            held((2, 256, 1024), BF16),
            held((256, 256), BF16),
            held((512, 256)),
            held((512, 768), BF16),
            held((4, 4, 2, 128), jnp.int32),
            held((1, 4), jnp.int32),
            held((4, 4, 2, 128), jnp.int32),
            held((1024, 512), BF16),
            held((2048, 512), BF16),
            held((1024, 512), BF16),
            held((1, 256)),
            held((32, 8, 256)),
            held((32, 8, 256)),
            held((2, 4, 2, 16, 256)),
            held((2, 4, 2, 16, 256)),
            held((32, 8, 256)),
            held((2, 4, 16, 256)),
            held((2, 4, 16, 256)),
            held((31, 8, 256)),
            held((16, 8, 256)),
            held((4, 2, 16, 256)),
            held((4, 2, 16, 256)),
            held((2, 16, 256)),
            held((16, 256)),
            held((16, 256)),
            dma((8,)),
            dma((3,)),
            dma((3,)),
            dma((2,)),
            dma((2,)),
            dma((13,)),
            dma((13,)),
            dma((4,)),
            dma((4,)),
            dma((4,)),
            dma((4,)),
            pltpu.SemaphoreType.REGULAR((7,)),
        ],
        compiler_params=pltpu.CompilerParams(
            vmem_limit_bytes=48 << 20, collective_id=0, has_side_effects=True
        ),
        name="window",
    )(*(pltpu.with_memory_space_constraint(a, pltpu.HBM) for a in given))
    new_embed, new_state, dest, rel_grad = pl.pallas_call(
        finish_kernel,
        out_shape=results,
        in_specs=[vmem] * 4,
        out_specs=[hbm] * 4,
        scratch_shapes=[dma((4,))],
        compiler_params=pltpu.CompilerParams(vmem_limit_bytes=4 << 20),
        name="finish",
    )(*found)
    return (new_embed, new_state.reshape(16), dest, rel_grad.reshape(512, 256))


def solution(mesh):
    return jax.shard_map(
        on_device,
        mesh=mesh,
        in_specs=(
            P("blk", None),
            P("blk"),
            P(),
            P("blk", "grp", None, None, None),
            P("blk", "grp", None, None, None),
            P("blk", "grp", None, None, None),
            P("blk", "grp", None, None, None),
            P("blk", "grp", None),
        ),
        out_specs=(P(("blk", "grp"), None), P(("blk", "grp")), P(("blk", "grp"), None), P()),
        check_vma=False,
    )
```

```python
import jax
import jax.numpy as jnp
from jax import lax
from jax.experimental import pallas as pl
from jax.experimental.pallas import tpu as pltpu
from jax.sharding import PartitionSpec as P

NZ = 16
NX = 4
NY = 8
NB = 64
MESH = pl.DeviceIdType.MESH
F32 = jnp.float32
BF16 = jnp.bfloat16


def position():
    b = lax.axis_index("blk")
    g = lax.axis_index("grp")
    z = lax.rem(b, NZ)
    y = lax.div(g, 8) * 4 + lax.div(b, NZ)
    x = lax.rem(lax.div(g, 2), NX)
    c = lax.rem(g, 2)
    return b, g, z, y, x, c


def at(z, y, x, c):
    return (lax.rem(y, 4) * NZ + z, lax.div(y, 4) * 8 + x * 2 + c)


def pairing(z, x):
    return x + lax.rem(z, 2) * (3 - 2 * x)


def remote(src, dst, send, recv, where):
    return pltpu.make_async_remote_copy(
        src_ref=src, dst_ref=dst, send_sem=send, recv_sem=recv, device_id=where, device_id_type=MESH
    )


def greet(where):
    pl.semaphore_signal(pltpu.get_barrier_semaphore(), inc=1, device_id=where, device_id_type=MESH)


def dot(a, b):
    return jnp.dot(a, b, preferred_element_type=F32)


def hot(hit):
    return jnp.where(hit, 1.0, 0.0).astype(BF16)


def columns_of(rows):
    turned = rows.T
    return jnp.concatenate([turned[:, 0:1], turned[:, 1:2]], axis=0)


def line_of(rows):
    return jnp.concatenate([rows[0:1], rows[1:2]], axis=1)


def split(ref, rows, value):
    top = value.astype(BF16)
    ref[rows, 0:256] = top
    ref[rows, 256:512] = (value - top.astype(F32)).astype(BF16)


def edge_gradients(slab, src_rows, rel_rows, pick_dst, pick_neg, scaled_grad, pos_grad, weight, g_rel):
    for k in range(NX):
        edges = slice(k * 256, k * 256 + 256)
        src_v = src_rows[edges]
        scaled = src_v * rel_rows[edges]
        dst_v = dot(pick_dst[edges], slab[...])
        neg_v = dot(pick_neg[edges], slab[...]).astype(BF16)
        positive = jnp.sum(scaled * dst_v, axis=1, keepdims=True)
        pull = -jax.nn.sigmoid(-positive)
        pos_grad[edges] = pull
        scaled_b = scaled.astype(BF16)
        from_neg = []
        for j in range(2):
            block = slice(j * 128, j * 128 + 128)
            s, n = scaled_b[block], neg_v[block]
            score = lax.dot_general(s, n, (((1,), (1,)), ((), ())), preferred_element_type=F32)
            push = (jax.nn.sigmoid(score) * (1.0 / 128.0)).astype(BF16)
            weight[k * 256 + j * 128 : k * 256 + j * 128 + 128] = push
            from_neg.append(dot(push, n))
        grad = pull * dst_v + jnp.concatenate(from_neg, axis=0)
        scaled_grad[edges] = grad
        split(g_rel, edges, grad * src_v)


def dst_gradients(src_rows, rel_rows, pos_grad, weight, g_dst):
    for k in range(NX):
        edges = slice(k * 256, k * 256 + 256)
        scaled = src_rows[edges] * rel_rows[edges]
        scaled_b = scaled.astype(BF16)
        split(g_dst, edges, pos_grad[edges] * scaled)
        for j in range(2):
            push = weight[k * 256 + j * 128 : k * 256 + j * 128 + 128]
            value = lax.dot_general(
                push, scaled_b[j * 128 : j * 128 + 128], (((0,), (0,)), ((), ())), preferred_element_type=F32
            )
            split(g_dst, slice(1024 + k * 256 + j * 128, 1024 + k * 256 + j * 128 + 128), value)


def src_gradients(rel_rows, scaled_grad, g_src):
    for k in range(NX):
        edges = slice(k * 256, k * 256 + 256)
        split(g_src, edges, scaled_grad[edges] * rel_rows[edges])


def both_terms(h, g):
    both = dot(h, g)
    return both[:, 0:256] + both[:, 256:512]


def window_kernel(
    embed,
    relation,
    src,
    dst,
    rel,
    neg,
    counts,
    state,
    new_embed,
    new_state,
    dest_out,
    rel_out,
    slab,
    index,
    src_rows,
    rel_rows,
    hot_src,
    hot_dst,
    hot_rel,
    own,
    table,
    parts,
    loaded,
    live,
    packed,
    g_src,
    g_dst,
    g_rel,
    pick_dst,
    pick_neg,
    scaled_grad,
    pos_grad,
    weight,
    own_state,
    rel_far,
    rel_near,
    src_part,
    dst_part,
    rel_pair,
    src_pair,
    dst_pair,
    rel_xy,
    rel_z,
    src_x,
    dst_x,
    src_half,
    src_y,
    dst_y,
    load_sem,
    idx_send,
    idx_recv,
    slab_send,
    slab_recv,
    send,
    recv,
    dst_send,
    dst_recv,
    pair_recv,
    all_recv,
    here,
):
    b, g, z, y, x, c = position()
    loads = [pltpu.make_async_copy(ref.at[0, 0], loaded.at[i], load_sem.at[i]) for i, ref in enumerate((src, dst, rel, neg))]
    loads.append(pltpu.make_async_copy(counts.at[0], live, load_sem.at[4]))
    load_own = pltpu.make_async_copy(embed, own, load_sem.at[5])
    load_table = pltpu.make_async_copy(relation, table, load_sem.at[6])
    load_state = pltpu.make_async_copy(state, own_state, load_sem.at[7])
    for copy in loads:
        copy.start()
    load_own.start()
    load_table.start()
    load_state.start()

    sibling = (b, g + 1 - 2 * c)
    turn = pairing(z, x)
    behind = (lax.rem(b + NB - turn, NB), g)
    wanted = [(s, pairing(z + s, x) == s, (lax.rem(b + s, NB), g)) for s in (3, 2, 1)]
    opposite = at(z, lax.rem(y + 4, NY), x, c)
    yh = lax.div(y, 4)
    base = lax.rem(b + 3 + NB - turn, NB)
    row_of = lax.div(g, 8) * 8 + c
    mine = x * NY + y

    y_order = (4, 3, 5, 2, 6, 1, 7, 0)
    z_offsets = (8, 7, 9, 6, 10, 5, 11, 4, 12, 3, 13, 2, 14, 1, 15)

    def plane(dx, dy):
        px, py = lax.rem(x + dx, NX), lax.rem(y + dy, NY)
        return px * NY + py, at(z, py, px, c)

    def along_x(d):
        return at(z, y, lax.rem(x + d, NX), c)

    def along_y(d):
        return at(z, lax.rem(y + NY + d, NY), x, c)

    def along_z(d):
        return at(lax.rem(z + NZ + d, NZ), y, x, c)

    def tell(i, *wheres):
        for where in wheres:
            pl.semaphore_signal(here.at[i], inc=1, device_id=where, device_id_type=MESH)

    greet(sibling)
    for d in (2, 1, 3):
        greet(along_x(d))
    for d in (1, -1):
        greet(along_y(d))
        greet(along_z(d))

    @pl.when(turn > 0)
    def _():
        greet(behind)

    for copy in loads:
        copy.wait()
    blocks = lax.broadcasted_iota(jnp.int32, (2, 128), 0)
    spots = lax.broadcasted_iota(jnp.int32, (1, 4), 1)
    for t in range(NX):
        count = jnp.sum(jnp.where(spots == t, live[...], 0), axis=1, keepdims=True)
        packed[t, 0] = jnp.where(blocks < count, loaded[0, t], -1)
        for i in range(1, 4):
            packed[t, i] = loaded[i, t]
    load_own.wait()
    pl.semaphore_wait(pltpu.get_barrier_semaphore(), 8 + sum(jnp.where(asked, 1, 0) for _, asked, _ in wanted))

    half = pl.ds(pl.multiple_of(c * 128, 128), 128)
    other = pl.ds(pl.multiple_of((1 - c) * 128, 128), 128)

    for s, asked, ahead in wanted:

        @pl.when(asked)
        def _():
            remote(own.at[half], slab.at[half], slab_send.at[s], slab_recv.at[0], ahead).start()

    sends = {}
    for d in (2, 1, 3):
        there = lax.rem(x + d, NX)
        sends[d] = remote(packed.at[pairing(z, there)], index.at[d], idx_send.at[d - 1], idx_recv.at[d - 1], along_x(d))
        sends[d].start()
    tell(0, along_y(1), along_y(-1))
    tell(1, along_z(1), along_z(-1))
    index[0:1] = packed[pl.ds(turn, 1)]

    @pl.when(turn == 0)
    def _():
        slab[...] = own[...]

    load_table.wait()
    r = table[...]
    high = r.astype(BF16)
    rest = r - high.astype(F32)
    middle = rest.astype(BF16)
    parts[:, 0:256] = high
    parts[:, 256:512] = middle
    parts[:, 512:768] = (rest - middle.astype(F32)).astype(BF16)

    lane = lax.broadcasted_iota(jnp.int32, (256, 256), 1)
    lane_r = lax.broadcasted_iota(jnp.int32, (256, 512), 1)
    sub = lax.broadcasted_iota(jnp.int32, (256, 256), 0)
    sub_r = lax.broadcasted_iota(jnp.int32, (2, 256, 256), 0) * 256 + lax.broadcasted_iota(jnp.int32, (2, 256, 256), 1)
    for k, d in enumerate((0, 1, 3, 2)):
        edges = slice(k * 256, k * 256 + 256)
        negs = slice(1024 + k * 256, 1024 + k * 256 + 256)
        if k == 1:
            pl.semaphore_wait(here.at[0], 2)
            pl.semaphore_wait(here.at[1], 2)
            tell(2, along_y(2), along_y(-2))
            tell(3, along_z(2), along_z(-2))
        if k == 2:
            pl.semaphore_wait(here.at[2], 2)
            pl.semaphore_wait(here.at[3], 2)
            tell(4, along_x(2), along_x(1), along_x(3))
            tell(5, along_z(4), along_z(-4))
        if k == 3:
            pl.semaphore_wait(here.at[4], 3)
            tell(6, along_z(-1), along_z(-2), along_z(-3))

        if d > 0:
            sends[d].wait_recv()
        src_rows[edges] = dot(hot(lane == columns_of(index[d, 0])), own[...])
        pieces = dot(hot(lane_r == columns_of(index[d, 2])), parts[...])
        rel_rows[edges] = (pieces[:, 0:256] + pieces[:, 256:512]) + pieces[:, 512:768]
        pick_dst[edges] = hot(lane == columns_of(index[d, 1]))
        pick_neg[edges] = hot(lane == columns_of(index[d, 3]))
        hot_src[:, edges] = hot(sub == line_of(index[d, 0]))
        hot_dst[:, edges] = hot(sub == line_of(index[d, 1]))
        hot_dst[:, negs] = hot(sub == line_of(index[d, 3]))
        hot_rel[:, :, edges] = hot(sub_r == line_of(index[d, 2])[None])

    @pl.when(turn > 0)
    def _():
        second = remote(slab.at[half], slab.at[half], slab_send.at[0], slab_recv.at[1], sibling)
        remote(own.at[half], slab.at[half], slab_send.at[0], slab_recv.at[0], sibling).wait_recv()
        second.start()
        remote(slab.at[other], slab.at[other], slab_send.at[0], slab_recv.at[1], sibling).wait_recv()
        second.wait_send()

    edge_gradients(slab, src_rows, rel_rows, pick_dst, pick_neg, scaled_grad, pos_grad, weight, g_rel)
    rel_far[...] = both_terms(hot_rel[pl.ds(1 - c, 1)][0], g_rel[...]).reshape(32, 8, 256)

    def pair(source, target, i):
        return remote(source, target, send.at[i], recv.at[i], sibling)

    src_c = pair(src_part.at[:, :, 1 - c], src_pair, 1)
    dst_c = pair(dst_part.at[:, :, 1 - c], dst_pair, 2)

    rel_c = {}
    for dx in (2, 1, 3, 0):
        rows = pl.ds(lax.rem(x + dx, NX) * NY, NY)
        rel_c[dx] = remote(rel_far.at[rows], rel_pair.at[rows], send.at[0], pair_recv.at[dx], sibling)
        rel_c[dx].start()
    rel_near[...] = both_terms(hot_rel[pl.ds(c, 1)][0], g_rel[...]).reshape(32, 8, 256)
    dst_gradients(src_rows, rel_rows, pos_grad, weight, g_dst)
    for dx in (2, 1, 3, 0):
        rows = pl.ds(lax.rem(x + dx, NX) * NY, NY)
        rel_c[dx].wait_recv()
        rel_near[rows] = rel_near[rows] + rel_pair[rows]
        for dy in y_order:
            if (dx, dy) != (0, 0):
                chunk, where = plane(dx, dy)
                remote(rel_near.at[chunk], rel_xy.at[(dx * NY + dy) - 1], send.at[3], recv.at[3], where).start()

    dst_part[...] = both_terms(hot_dst[...], g_dst[...]).reshape(2, 4, 2, 16, 256)
    dst_c.start()
    src_gradients(rel_rows, scaled_grad, g_src)
    src_part[...] = both_terms(hot_src[...], g_src[...]).reshape(2, 4, 2, 16, 256)
    dst_c.wait_recv()
    dst_pair[...] = dst_pair[...] + dst_part[:, :, pl.ds(c, 1)].reshape(2, 4, 16, 256)
    pl.semaphore_wait(here.at[6], 3)
    for px in range(NX):
        to = (base, row_of + 2 * px)

        @pl.when(jnp.logical_or(turn != 3, x != px))
        def _():
            remote(dst_pair.at[:, px], dst_x.at[turn], dst_send.at[px], dst_recv.at[turn], to).start()

    @pl.when(turn == 3)
    def _():
        dst_x[3:4] = dst_pair[:, pl.ds(x, 1)].reshape(1, 2, 16, 256)

    src_c.start()

    offsets = [(dx, dy) for dx in (2, 1, 3, 0) for dy in y_order if (dx, dy) != (0, 0)]

    def chunks(ref, n, sem):
        return pltpu.make_async_copy(ref.at[pl.ds(0, n)], ref.at[pl.ds(0, n)], sem)

    chunks(rel_xy, 31, recv.at[3]).wait()
    rel_z[pl.ds(z, 1)] = (rel_near[pl.ds(mine, 1)][0] + jnp.sum(rel_xy[...], axis=0))[None]
    pl.semaphore_wait(here.at[5], 2)
    for dz in z_offsets:
        where = along_z(dz)
        remote(rel_z.at[z], rel_z.at[z], send.at[8], recv.at[8], where).start()

    src_c.wait_recv()
    src_pair[...] = src_pair[...] + src_part[:, :, pl.ds(c, 1)].reshape(2, 4, 16, 256)
    src_sends = []
    for d in (2, 1, 3):
        px = lax.rem(x + d, NX)
        copy = remote(src_pair.at[:, px], src_x.at[d], send.at[4 + d], recv.at[4 + d], at(z, y, px, c))
        copy.start()
        src_sends.append(copy)
    for copy in src_sends:
        copy.wait_recv()
    src_half[...] = (src_pair[:, pl.ds(x, 1)].reshape(2, 16, 256) + src_x[1]) + (src_x[2] + src_x[3])
    src_far = remote(src_half.at[1 - yh], src_y, send.at[9], recv.at[9], opposite)
    src_far.start()
    for t in range(NX):

        @pl.when(jnp.logical_or(turn != 3, t != 3))
        def _():
            remote(dst_pair.at[:, t], dst_x.at[t], dst_send.at[t], dst_recv.at[t], sibling).wait_recv()

    dst_x[0] = (dst_x[0] + dst_x[1]) + (dst_x[2] + dst_x[3])
    dst_far = remote(dst_x.at[0, 1 - yh], dst_y, send.at[10], recv.at[10], opposite)
    dst_far.start()
    chunks(rel_z, 15, recv.at[8]).wait()
    rel_out[pl.ds(c, 1), pl.ds(mine, 1)] = jnp.sum(rel_z[...], axis=0)[None, None]
    for dx, dy in offsets:
        _, where = plane(dx, dy)
        remote(rel_out.at[c, mine], rel_out.at[c, mine], send.at[11], all_recv.at[dx], where).start()
    load_state.wait()
    src_far.wait_recv()
    total = src_half[pl.ds(yh, 1)][0] + src_y[...]
    lane = lax.broadcasted_iota(jnp.int32, (16, 256), 1)
    line = lax.broadcasted_iota(jnp.int32, (16, 256), 0)
    old = jnp.sum(jnp.where(lane == line + g * 16, own_state[...], 0.0), axis=1, keepdims=True)
    fresh = old + jnp.sum(total * total, axis=1, keepdims=True) * (1.0 / 256.0)
    new_embed[...] = own[pl.ds(pl.multiple_of(g * 16, 16), 16)].astype(F32) - 0.5 * total / jnp.sqrt(fresh)
    lane16 = lax.broadcasted_iota(jnp.int32, (16, 16), 1)
    line16 = lax.broadcasted_iota(jnp.int32, (16, 16), 0)
    new_state[...] = jnp.sum(jnp.where(lane16 == line16, fresh, 0.0), axis=0, keepdims=True)
    for dx in (0, 1, 3, 2):
        chunks(rel_xy, 7 if dx == 0 else 8, all_recv.at[dx]).wait()
        group = pl.ds(lax.rem(x + NX - dx, NX) * NY, NY)
        remote(rel_out.at[c, group], rel_out.at[c, group], send.at[12], recv.at[12], sibling).start()
    dst_far.wait_recv()
    dest_out[...] = dst_x[0, pl.ds(yh, 1)].reshape(16, 256) + dst_y[...]
    for d in (1, 2, 3):
        sends[d].wait_send()
    for s, asked, ahead in wanted:

        @pl.when(asked)
        def _():
            remote(own.at[half], slab.at[half], slab_send.at[s], slab_recv.at[0], ahead).wait_send()

    remote(rel_far, rel_pair, send.at[0], recv.at[0], sibling).wait_send()
    src_c.wait_send()
    dst_c.wait_send()
    chunks(rel_xy, 31, send.at[3]).wait()
    chunks(rel_z, 15, send.at[8]).wait()
    chunks(rel_xy, 31, send.at[11]).wait()
    for copy in src_sends:
        copy.wait_send()
    for px in range(NX):

        @pl.when(jnp.logical_or(turn != 3, x != px))
        def _():
            remote(dst_pair.at[:, px], dst_x.at[0], dst_send.at[px], dst_recv.at[0], sibling).wait_send()

    src_far.wait_send()
    dst_far.wait_send()
    last = remote(rel_out.at[c], rel_out.at[c], send.at[12], recv.at[12], sibling)
    last.wait_send()
    remote(rel_out.at[1 - c], rel_out.at[1 - c], send.at[12], recv.at[12], sibling).wait_recv()


def finish_kernel(a, b, c, d, a_out, b_out, c_out, d_out, sem):
    copies = [
        pltpu.make_async_copy(held, out, sem.at[i])
        for i, (held, out) in enumerate(((d, d_out), (a, a_out), (c, c_out), (b, b_out)))
    ]
    for copy in copies:
        copy.start()
    for copy in copies:
        copy.wait()


def on_device(embed, state, relation, src_index, dst_index, rel_index, neg_index, counts):
    vmem = pl.BlockSpec(memory_space=pltpu.VMEM)
    hbm = pl.BlockSpec(memory_space=pltpu.HBM)
    dma = pltpu.SemaphoreType.DMA

    def held(dims, kind=F32):
        return pltpu.VMEM(dims, kind)

    results = [
        jax.ShapeDtypeStruct(dims, F32) for dims in ((16, 256), (1, 16), (16, 256), (2, 32, 8, 256))
    ]
    given = (embed, relation, src_index, dst_index, rel_index, neg_index, counts, state.reshape(1, 256))
    found = pl.pallas_call(
        window_kernel,
        out_shape=results,
        in_specs=[hbm] * 8,
        out_specs=[vmem] * 4,
        scratch_shapes=[
            held((256, 256), BF16),
            held((4, 4, 2, 128), jnp.int32),
            held((1024, 256)),
            held((1024, 256)),
            held((256, 1024), BF16),
            held((256, 2048), BF16),
            held((2, 256, 1024), BF16),
            held((256, 256), BF16),
            held((512, 256)),
            held((512, 768), BF16),
            held((4, 4, 2, 128), jnp.int32),
            held((1, 4), jnp.int32),
            held((4, 4, 2, 128), jnp.int32),
            held((1024, 512), BF16),
            held((2048, 512), BF16),
            held((1024, 512), BF16),
            held((1024, 256), BF16),
            held((1024, 256), BF16),
            held((1024, 256)),
            held((1024, 1)),
            held((1024, 128), BF16),
            held((1, 256)),
            held((32, 8, 256)),
            held((32, 8, 256)),
            held((2, 4, 2, 16, 256)),
            held((2, 4, 2, 16, 256)),
            held((32, 8, 256)),
            held((2, 4, 16, 256)),
            held((2, 4, 16, 256)),
            held((31, 8, 256)),
            held((16, 8, 256)),
            held((4, 2, 16, 256)),
            held((4, 2, 16, 256)),
            held((2, 16, 256)),
            held((16, 256)),
            held((16, 256)),
            dma((8,)),
            dma((3,)),
            dma((3,)),
            dma((4,)),
            dma((2,)),
            dma((13,)),
            dma((13,)),
            dma((4,)),
            dma((4,)),
            dma((4,)),
            dma((4,)),
            pltpu.SemaphoreType.REGULAR((7,)),
        ],
        compiler_params=pltpu.CompilerParams(
            vmem_limit_bytes=48 << 20, collective_id=0, has_side_effects=True
        ),
        name="window",
    )(*(pltpu.with_memory_space_constraint(a, pltpu.HBM) for a in given))
    new_embed, new_state, dest, rel_grad = pl.pallas_call(
        finish_kernel,
        out_shape=results,
        in_specs=[vmem] * 4,
        out_specs=[hbm] * 4,
        scratch_shapes=[dma((4,))],
        compiler_params=pltpu.CompilerParams(vmem_limit_bytes=4 << 20),
        name="finish",
    )(*found)
    return (new_embed, new_state.reshape(16), dest, rel_grad.reshape(512, 256))


def solution(mesh):
    return jax.shard_map(
        on_device,
        mesh=mesh,
        in_specs=(
            P("blk", None),
            P("blk"),
            P(),
            P("blk", "grp", None, None, None),
            P("blk", "grp", None, None, None),
            P("blk", "grp", None, None, None),
            P("blk", "grp", None, None, None),
            P("blk", "grp", None),
        ),
        out_specs=(P(("blk", "grp"), None), P(("blk", "grp")), P(("blk", "grp"), None), P()),
        check_vma=False,
    )
```

```python
import jax
import jax.numpy as jnp
from jax import lax
from jax.experimental import pallas as pl
from jax.experimental.pallas import tpu as pltpu
from jax.sharding import PartitionSpec as P

NZ = 16
NX = 4
NY = 8
NB = 64
MESH = pl.DeviceIdType.MESH
F32 = jnp.float32
BF16 = jnp.bfloat16


def position():
    b = lax.axis_index("blk")
    g = lax.axis_index("grp")
    z = lax.rem(b, NZ)
    y = lax.div(g, 8) * 4 + lax.div(b, NZ)
    x = lax.rem(lax.div(g, 2), NX)
    c = lax.rem(g, 2)
    return b, g, z, y, x, c


def at(z, y, x, c):
    return (lax.rem(y, 4) * NZ + z, lax.div(y, 4) * 8 + x * 2 + c)


def pairing(z, x):
    return x + lax.rem(z, 2) * (3 - 2 * x)


def remote(src, dst, send, recv, where):
    return pltpu.make_async_remote_copy(
        src_ref=src, dst_ref=dst, send_sem=send, recv_sem=recv, device_id=where, device_id_type=MESH
    )


def greet(where):
    pl.semaphore_signal(pltpu.get_barrier_semaphore(), inc=1, device_id=where, device_id_type=MESH)


def dot(a, b):
    return jnp.dot(a, b, preferred_element_type=F32)


def hot(hit):
    return jnp.where(hit, 1.0, 0.0).astype(BF16)


def columns_of(rows):
    turned = rows.T
    return jnp.concatenate([turned[:, 0:1], turned[:, 1:2]], axis=0)


def line_of(rows):
    return jnp.concatenate([rows[0:1], rows[1:2]], axis=1)


def split(ref, rows, value):
    top = value.astype(BF16)
    ref[rows, 0:256] = top
    ref[rows, 256:512] = (value - top.astype(F32)).astype(BF16)


def split_halves(ref, rows, value):
    top = value.astype(BF16)
    low = (value - top.astype(F32)).astype(BF16)
    for h in range(2):
        ref[rows, 256 * h : 256 * h + 128] = top[:, 128 * h : 128 * h + 128]
        ref[rows, 256 * h + 128 : 256 * h + 256] = low[:, 128 * h : 128 * h + 128]


def edge_gradients(slab, src_rows, rel_rows, pick_dst, pick_neg, scaled_grad, pos_grad, weight, g_rel):
    for k in range(NX):
        edges = slice(k * 256, k * 256 + 256)
        src_v = src_rows[edges]
        scaled = src_v * rel_rows[edges]
        dst_v = dot(pick_dst[edges], slab[...])
        neg_v = dot(pick_neg[edges], slab[...]).astype(BF16)
        positive = jnp.sum(scaled * dst_v, axis=1, keepdims=True)
        pull = -jax.nn.sigmoid(-positive)
        pos_grad[edges] = pull
        scaled_b = scaled.astype(BF16)
        from_neg = []
        for j in range(2):
            block = slice(j * 128, j * 128 + 128)
            s, n = scaled_b[block], neg_v[block]
            score = lax.dot_general(s, n, (((1,), (1,)), ((), ())), preferred_element_type=F32)
            push = (jax.nn.sigmoid(score) * (1.0 / 128.0)).astype(BF16)
            weight[k * 256 + j * 128 : k * 256 + j * 128 + 128] = push
            from_neg.append(dot(push, n))
        grad = pull * dst_v + jnp.concatenate(from_neg, axis=0)
        scaled_grad[edges] = grad
        split_halves(g_rel, edges, grad * src_v)


def dst_gradients(src_rows, rel_rows, pos_grad, weight, g_dst):
    for k in range(NX):
        edges = slice(k * 256, k * 256 + 256)
        scaled = src_rows[edges] * rel_rows[edges]
        scaled_b = scaled.astype(BF16)
        split(g_dst, edges, pos_grad[edges] * scaled)
        for j in range(2):
            push = weight[k * 256 + j * 128 : k * 256 + j * 128 + 128]
            value = lax.dot_general(
                push, scaled_b[j * 128 : j * 128 + 128], (((0,), (0,)), ((), ())), preferred_element_type=F32
            )
            split(g_dst, slice(1024 + k * 256 + j * 128, 1024 + k * 256 + j * 128 + 128), value)


def src_gradients(rel_rows, scaled_grad, g_src):
    for k in range(NX):
        edges = slice(k * 256, k * 256 + 256)
        split(g_src, edges, scaled_grad[edges] * rel_rows[edges])


def both_terms(h, g):
    both = dot(h, g)
    return both[:, 0:256] + both[:, 256:512]


def window_kernel(
    embed,
    relation,
    src,
    dst,
    rel,
    neg,
    counts,
    state,
    new_embed,
    new_state,
    dest_out,
    rel_out,
    slab,
    index,
    src_rows,
    rel_rows,
    hot_src,
    hot_dst,
    hot_rel,
    own,
    table,
    parts,
    loaded,
    live,
    packed,
    g_src,
    g_dst,
    g_rel,
    pick_dst,
    pick_neg,
    scaled_grad,
    pos_grad,
    weight,
    own_state,
    rel_far,
    rel_near,
    src_part,
    dst_part,
    rel_pair,
    src_pair,
    dst_pair,
    rel_xy,
    rel_z,
    src_x,
    dst_x,
    src_half,
    dst_half,
    src_y,
    dst_y,
    load_sem,
    idx_send,
    idx_recv,
    slab_send,
    slab_recv,
    send,
    recv,
    dst_send,
    dst_recv,
    pair_recv,
    xy_recv,
    z_recv,
    all_recv,
    here,
):
    b, g, z, y, x, c = position()
    loads = [pltpu.make_async_copy(ref.at[0, 0], loaded.at[i], load_sem.at[i]) for i, ref in enumerate((src, dst, rel, neg))]
    loads.append(pltpu.make_async_copy(counts.at[0], live, load_sem.at[4]))
    load_own = pltpu.make_async_copy(embed, own, load_sem.at[5])
    load_table = pltpu.make_async_copy(relation, table, load_sem.at[6])
    load_state = pltpu.make_async_copy(state, own_state, load_sem.at[7])
    for copy in loads:
        copy.start()
    load_own.start()
    load_table.start()
    load_state.start()

    sibling = (b, g + 1 - 2 * c)
    turn = pairing(z, x)
    behind = (lax.rem(b + NB - turn, NB), g)
    wanted = [(s, pairing(z + s, x) == s, (lax.rem(b + s, NB), g)) for s in (3, 2, 1)]
    opposite = at(z, lax.rem(y + 4, NY), x, c)
    yh = lax.div(y, 4)
    base = lax.rem(b + 3 + NB - turn, NB)
    row_of = lax.div(g, 8) * 8 + c
    mine = x * NY + y

    y_order = (4, 3, 5, 2, 6, 1, 7, 0)
    z_offsets = (8, 7, 9, 6, 10, 5, 11, 4, 12, 3, 13, 2, 14, 1, 15)

    def plane(dx, dy):
        px, py = lax.rem(x + dx, NX), lax.rem(y + dy, NY)
        return px * NY + py, at(z, py, px, c)

    def along_x(d):
        return at(z, y, lax.rem(x + d, NX), c)

    def along_y(d):
        return at(z, lax.rem(y + NY + d, NY), x, c)

    def along_z(d):
        return at(lax.rem(z + NZ + d, NZ), y, x, c)

    def tell(i, *wheres):
        for where in wheres:
            pl.semaphore_signal(here.at[i], inc=1, device_id=where, device_id_type=MESH)

    greet(sibling)
    for d in (2, 1, 3):
        greet(along_x(d))
    for d in (1, -1):
        greet(along_y(d))
        greet(along_z(d))

    @pl.when(turn > 0)
    def _():
        greet(behind)

    for copy in loads:
        copy.wait()
    blocks = lax.broadcasted_iota(jnp.int32, (2, 128), 0)
    spots = lax.broadcasted_iota(jnp.int32, (1, 4), 1)
    for t in range(NX):
        count = jnp.sum(jnp.where(spots == t, live[...], 0), axis=1, keepdims=True)
        packed[t, 0] = jnp.where(blocks < count, loaded[0, t], -1)
        for i in range(1, 4):
            packed[t, i] = loaded[i, t]
    load_own.wait()
    pl.semaphore_wait(pltpu.get_barrier_semaphore(), 8 + sum(jnp.where(asked, 1, 0) for _, asked, _ in wanted))

    half = pl.ds(pl.multiple_of(c * 128, 128), 128)
    other = pl.ds(pl.multiple_of((1 - c) * 128, 128), 128)

    for s, asked, ahead in wanted:

        @pl.when(asked)
        def _():
            remote(own.at[half], slab.at[half], slab_send.at[s], slab_recv.at[0], ahead).start()

    sends = {}
    for d in (2, 1, 3):
        there = lax.rem(x + d, NX)
        sends[d] = remote(packed.at[pairing(z, there)], index.at[d], idx_send.at[d - 1], idx_recv.at[d - 1], along_x(d))
        sends[d].start()
    tell(0, along_y(1), along_y(-1))
    tell(1, along_z(1), along_z(-1))
    index[0:1] = packed[pl.ds(turn, 1)]

    @pl.when(turn == 0)
    def _():
        slab[...] = own[...]

    load_table.wait()
    r = table[...]
    high = r.astype(BF16)
    rest = r - high.astype(F32)
    middle = rest.astype(BF16)
    parts[:, 0:256] = high
    parts[:, 256:512] = middle
    parts[:, 512:768] = (rest - middle.astype(F32)).astype(BF16)

    lane = lax.broadcasted_iota(jnp.int32, (256, 256), 1)
    lane_r = lax.broadcasted_iota(jnp.int32, (256, 512), 1)
    sub = lax.broadcasted_iota(jnp.int32, (256, 256), 0)
    sub_r = lax.broadcasted_iota(jnp.int32, (2, 256, 256), 0) * 256 + lax.broadcasted_iota(jnp.int32, (2, 256, 256), 1)
    for k, d in enumerate((0, 1, 3, 2)):
        edges = slice(k * 256, k * 256 + 256)
        negs = slice(1024 + k * 256, 1024 + k * 256 + 256)
        if k == 1:
            pl.semaphore_wait(here.at[0], 2)
            pl.semaphore_wait(here.at[1], 2)
            tell(2, along_y(2), along_y(-2))
            tell(3, along_z(2), along_z(-2))
        if k == 2:
            pl.semaphore_wait(here.at[2], 2)
            pl.semaphore_wait(here.at[3], 2)
            tell(4, along_x(2), along_x(1), along_x(3))
            tell(5, along_z(4), along_z(-4))
        if k == 3:
            pl.semaphore_wait(here.at[4], 3)
            tell(6, along_z(-1), along_z(-2), along_z(-3))

        if d > 0:
            sends[d].wait_recv()
        src_rows[edges] = dot(hot(lane == columns_of(index[d, 0])), own[...])
        pieces = dot(hot(lane_r == columns_of(index[d, 2])), parts[...])
        rel_rows[edges] = (pieces[:, 0:256] + pieces[:, 256:512]) + pieces[:, 512:768]
        pick_dst[edges] = hot(lane == columns_of(index[d, 1]))
        pick_neg[edges] = hot(lane == columns_of(index[d, 3]))
        hot_src[:, edges] = hot(sub == line_of(index[d, 0]))
        hot_dst[:, edges] = hot(sub == line_of(index[d, 1]))
        hot_dst[:, negs] = hot(sub == line_of(index[d, 3]))
        hot_rel[:, :, edges] = hot(sub_r == line_of(index[d, 2])[None])

    @pl.when(turn > 0)
    def _():
        second = remote(slab.at[half], slab.at[half], slab_send.at[0], slab_recv.at[1], sibling)
        remote(own.at[half], slab.at[half], slab_send.at[0], slab_recv.at[0], sibling).wait_recv()
        second.start()
        remote(slab.at[other], slab.at[other], slab_send.at[0], slab_recv.at[1], sibling).wait_recv()
        second.wait_send()

    edge_gradients(slab, src_rows, rel_rows, pick_dst, pick_neg, scaled_grad, pos_grad, weight, g_rel)
    def pair(source, target, i):
        return remote(source, target, send.at[i], recv.at[i], sibling)

    def chunks(n, sem):
        return pltpu.make_async_copy(rel_xy.at[0, pl.ds(0, n)], rel_xy.at[0, pl.ds(0, n)], sem)

    def half_terms(core, h):
        both = dot(hot_rel[pl.ds(core, 1)][0], g_rel[:, 256 * h : 256 * h + 256])
        return (both[:, 0:128] + both[:, 128:256]).reshape(32, 8, 128)

    src_c = pair(src_part.at[:, :, 1 - c], src_pair, 1)
    dst_c = pair(dst_part.at[:, :, 1 - c], dst_pair, 2)
    offsets = [(dx, dy) for dx in (2, 1, 3, 0) for dy in y_order if (dx, dy) != (0, 0)]

    rel_c = [remote(rel_far.at[h], rel_pair.at[h], send.at[0], pair_recv.at[h], sibling) for h in range(2)]
    for h in range(2):
        rel_far[h] = half_terms(1 - c, h)
        rel_c[h].start()
    for h in range(2):
        rel_near[h] = half_terms(c, h)
    rel_c[0].wait_recv()
    rel_near[0] = rel_near[0] + rel_pair[0]
    for i, (dx, dy) in enumerate(offsets):
        chunk, where = plane(dx, dy)
        remote(rel_near.at[0, chunk], rel_xy.at[0, i], send.at[3], xy_recv.at[0], where).start()
    dst_gradients(src_rows, rel_rows, pos_grad, weight, g_dst)
    dst_part[...] = both_terms(hot_dst[...], g_dst[...]).reshape(2, 4, 2, 16, 256)
    dst_c.start()
    rel_c[1].wait_recv()
    rel_near[1] = rel_near[1] + rel_pair[1]
    for i, (dx, dy) in enumerate(offsets):
        chunk, where = plane(dx, dy)
        remote(rel_near.at[1, chunk], rel_xy.at[1, i], send.at[3], xy_recv.at[1], where).start()

    dst_c.wait_recv()
    dst_pair[...] = dst_pair[...] + dst_part[:, :, pl.ds(c, 1)].reshape(2, 4, 16, 256)
    dst_far = remote(dst_pair.at[1 - yh], dst_y, send.at[10], recv.at[10], opposite)
    src_gradients(rel_rows, scaled_grad, g_src)
    src_part[...] = both_terms(hot_src[...], g_src[...]).reshape(2, 4, 2, 16, 256)
    src_c.start()

    pl.semaphore_wait(here.at[5], 2)
    for h in range(2):
        chunks(31, xy_recv.at[h]).wait()
        rel_z[h, pl.ds(z, 1)] = (rel_near[h, pl.ds(mine, 1)][0] + jnp.sum(rel_xy[h], axis=0))[None]
        for dz in z_offsets:
            remote(rel_z.at[h, z], rel_z.at[h, z], send.at[8], z_recv.at[h], along_z(dz)).start()
        if h == 0:
            dst_far.start()

    src_c.wait_recv()
    src_pair[...] = src_pair[...] + src_part[:, :, pl.ds(c, 1)].reshape(2, 4, 16, 256)
    src_sends = []
    for d in (2, 1, 3):
        px = lax.rem(x + d, NX)
        copy = remote(src_pair.at[:, px], src_x.at[d], send.at[4 + d], recv.at[4 + d], at(z, y, px, c))
        copy.start()
        src_sends.append(copy)
    for copy in src_sends:
        copy.wait_recv()
    src_half[...] = (src_pair[:, pl.ds(x, 1)].reshape(2, 16, 256) + src_x[1]) + (src_x[2] + src_x[3])
    src_far = remote(src_half.at[1 - yh], src_y, send.at[9], recv.at[9], opposite)
    src_far.start()

    dst_far.wait_recv()
    dst_half[...] = dst_pair[pl.ds(yh, 1)][0] + dst_y[...]
    pl.semaphore_wait(here.at[6], 3)
    for px in range(NX):
        to = (base, row_of + 2 * px)

        @pl.when(jnp.logical_or(turn != 3, x != px))
        def _():
            remote(dst_half.at[px], dst_x.at[turn], dst_send.at[px], dst_recv.at[turn], to).start()

    @pl.when(turn == 3)
    def _():
        dst_x[3:4] = dst_half[pl.ds(x, 1)]

    for h in range(2):
        cols = slice(128 * h, 128 * h + 128)
        chunks(15, z_recv.at[h]).wait()
        rel_out[pl.ds(c, 1), pl.ds(mine, 1), :, cols] = jnp.sum(rel_z[h], axis=0)[None, None]
        for dx, dy in offsets:
            _, where = plane(dx, dy)
            out = rel_out.at[c, mine, :, cols]
            remote(out, out, send.at[11], all_recv.at[h, dx], where).start()

    load_state.wait()
    src_far.wait_recv()
    total = src_half[pl.ds(yh, 1)][0] + src_y[...]
    lane = lax.broadcasted_iota(jnp.int32, (16, 256), 1)
    line = lax.broadcasted_iota(jnp.int32, (16, 256), 0)
    old = jnp.sum(jnp.where(lane == line + g * 16, own_state[...], 0.0), axis=1, keepdims=True)
    fresh = old + jnp.sum(total * total, axis=1, keepdims=True) * (1.0 / 256.0)
    new_embed[...] = own[pl.ds(pl.multiple_of(g * 16, 16), 16)].astype(F32) - 0.5 * total / jnp.sqrt(fresh)
    lane16 = lax.broadcasted_iota(jnp.int32, (16, 16), 1)
    line16 = lax.broadcasted_iota(jnp.int32, (16, 16), 0)
    new_state[...] = jnp.sum(jnp.where(lane16 == line16, fresh, 0.0), axis=0, keepdims=True)

    for h in range(2):
        for dx in (0, 1, 3, 2):
            chunks(7 if dx == 0 else 8, all_recv.at[h, dx]).wait()
            group = rel_out.at[c, pl.ds(lax.rem(x + NX - dx, NX) * NY, NY), :, 128 * h : 128 * h + 128]
            remote(group, group, send.at[12], recv.at[12], sibling).start()
    for t in range(NX):

        @pl.when(jnp.logical_or(turn != 3, t != 3))
        def _():
            remote(dst_half.at[t], dst_x.at[t], dst_send.at[t], dst_recv.at[t], sibling).wait_recv()

    dest_out[...] = (dst_x[0] + dst_x[1]) + (dst_x[2] + dst_x[3])
    for d in (1, 2, 3):
        sends[d].wait_send()
    for s, asked, ahead in wanted:

        @pl.when(asked)
        def _():
            remote(own.at[half], slab.at[half], slab_send.at[s], slab_recv.at[0], ahead).wait_send()

    remote(rel_far, rel_pair, send.at[0], recv.at[0], sibling).wait_send()
    src_c.wait_send()
    dst_c.wait_send()
    for _ in range(2):
        chunks(31, send.at[3]).wait()
        chunks(15, send.at[8]).wait()
        chunks(31, send.at[11]).wait()
    for copy in src_sends:
        copy.wait_send()
    for px in range(NX):

        @pl.when(jnp.logical_or(turn != 3, x != px))
        def _():
            remote(dst_half.at[px], dst_x.at[0], dst_send.at[px], dst_recv.at[0], sibling).wait_send()

    src_far.wait_send()
    dst_far.wait_send()
    last = remote(rel_out.at[c], rel_out.at[c], send.at[12], recv.at[12], sibling)
    last.wait_send()
    remote(rel_out.at[1 - c], rel_out.at[1 - c], send.at[12], recv.at[12], sibling).wait_recv()


def finish_kernel(a, b, c, d, a_out, b_out, c_out, d_out, sem):
    copies = [
        pltpu.make_async_copy(held, out, sem.at[i])
        for i, (held, out) in enumerate(((d, d_out), (a, a_out), (c, c_out), (b, b_out)))
    ]
    for copy in copies:
        copy.start()
    for copy in copies:
        copy.wait()


def on_device(embed, state, relation, src_index, dst_index, rel_index, neg_index, counts):
    vmem = pl.BlockSpec(memory_space=pltpu.VMEM)
    hbm = pl.BlockSpec(memory_space=pltpu.HBM)
    dma = pltpu.SemaphoreType.DMA

    def held(dims, kind=F32):
        return pltpu.VMEM(dims, kind)

    results = [
        jax.ShapeDtypeStruct(dims, F32) for dims in ((16, 256), (1, 16), (16, 256), (2, 32, 8, 256))
    ]
    given = (embed, relation, src_index, dst_index, rel_index, neg_index, counts, state.reshape(1, 256))
    found = pl.pallas_call(
        window_kernel,
        out_shape=results,
        in_specs=[hbm] * 8,
        out_specs=[vmem] * 4,
        scratch_shapes=[
            held((256, 256), BF16),
            held((4, 4, 2, 128), jnp.int32),
            held((1024, 256)),
            held((1024, 256)),
            held((256, 1024), BF16),
            held((256, 2048), BF16),
            held((2, 256, 1024), BF16),
            held((256, 256), BF16),
            held((512, 256)),
            held((512, 768), BF16),
            held((4, 4, 2, 128), jnp.int32),
            held((1, 4), jnp.int32),
            held((4, 4, 2, 128), jnp.int32),
            held((1024, 512), BF16),
            held((2048, 512), BF16),
            held((1024, 512), BF16),
            held((1024, 256), BF16),
            held((1024, 256), BF16),
            held((1024, 256)),
            held((1024, 1)),
            held((1024, 128), BF16),
            held((1, 256)),
            held((2, 32, 8, 128)),
            held((2, 32, 8, 128)),
            held((2, 4, 2, 16, 256)),
            held((2, 4, 2, 16, 256)),
            held((2, 32, 8, 128)),
            held((2, 4, 16, 256)),
            held((2, 4, 16, 256)),
            held((2, 31, 8, 128)),
            held((2, 16, 8, 128)),
            held((4, 2, 16, 256)),
            held((4, 16, 256)),
            held((2, 16, 256)),
            held((4, 16, 256)),
            held((16, 256)),
            held((4, 16, 256)),
            dma((8,)),
            dma((3,)),
            dma((3,)),
            dma((4,)),
            dma((2,)),
            dma((13,)),
            dma((13,)),
            dma((4,)),
            dma((4,)),
            dma((2,)),
            dma((2,)),
            dma((2,)),
            dma((2, 4)),
            pltpu.SemaphoreType.REGULAR((7,)),
        ],
        compiler_params=pltpu.CompilerParams(
            vmem_limit_bytes=48 << 20, collective_id=0, has_side_effects=True
        ),
        name="window",
    )(*(pltpu.with_memory_space_constraint(a, pltpu.HBM) for a in given))
    new_embed, new_state, dest, rel_grad = pl.pallas_call(
        finish_kernel,
        out_shape=results,
        in_specs=[vmem] * 4,
        out_specs=[hbm] * 4,
        scratch_shapes=[dma((4,))],
        compiler_params=pltpu.CompilerParams(vmem_limit_bytes=4 << 20),
        name="finish",
    )(*found)
    return (new_embed, new_state.reshape(16), dest, rel_grad.reshape(512, 256))


def solution(mesh):
    return jax.shard_map(
        on_device,
        mesh=mesh,
        in_specs=(
            P("blk", None),
            P("blk"),
            P(),
            P("blk", "grp", None, None, None),
            P("blk", "grp", None, None, None),
            P("blk", "grp", None, None, None),
            P("blk", "grp", None, None, None),
            P("blk", "grp", None),
        ),
        out_specs=(P(("blk", "grp"), None), P(("blk", "grp")), P(("blk", "grp"), None), P()),
        check_vma=False,
    )
```

```python
import jax
import jax.numpy as jnp
from jax import lax
from jax.experimental import pallas as pl
from jax.experimental.pallas import tpu as pltpu
from jax.sharding import PartitionSpec as P

NZ = 16
NX = 4
NY = 8
NB = 64
MESH = pl.DeviceIdType.MESH
F32 = jnp.float32
BF16 = jnp.bfloat16


def position():
    b = lax.axis_index("blk")
    g = lax.axis_index("grp")
    z = lax.rem(b, NZ)
    y = lax.div(g, 8) * 4 + lax.div(b, NZ)
    x = lax.rem(lax.div(g, 2), NX)
    c = lax.rem(g, 2)
    return b, g, z, y, x, c


def at(z, y, x, c):
    return (lax.rem(y, 4) * NZ + z, lax.div(y, 4) * 8 + x * 2 + c)


def pairing(z, x):
    return x + lax.rem(z, 2) * (3 - 2 * x)


def remote(src, dst, send, recv, where):
    return pltpu.make_async_remote_copy(
        src_ref=src, dst_ref=dst, send_sem=send, recv_sem=recv, device_id=where, device_id_type=MESH
    )


def greet(where):
    pl.semaphore_signal(pltpu.get_barrier_semaphore(), inc=1, device_id=where, device_id_type=MESH)


def dot(a, b):
    return jnp.dot(a, b, preferred_element_type=F32)


def hot(hit):
    return jnp.where(hit, 1.0, 0.0).astype(BF16)


def columns_of(rows):
    turned = rows.T
    return jnp.concatenate([turned[:, 0:1], turned[:, 1:2]], axis=0)


def line_of(rows):
    return jnp.concatenate([rows[0:1], rows[1:2]], axis=1)


def split(ref, rows, value):
    top = value.astype(BF16)
    ref[rows, 0:256] = top
    ref[rows, 256:512] = (value - top.astype(F32)).astype(BF16)


def split_halves(ref, rows, value):
    top = value.astype(BF16)
    low = (value - top.astype(F32)).astype(BF16)
    for h in range(2):
        ref[rows, 256 * h : 256 * h + 128] = top[:, 128 * h : 128 * h + 128]
        ref[rows, 256 * h + 128 : 256 * h + 256] = low[:, 128 * h : 128 * h + 128]


def edge_gradients(slab, src_rows, rel_rows, pick_dst, pick_neg, scaled_grad, pos_grad, weight, g_rel):
    for k in range(NX):
        edges = slice(k * 256, k * 256 + 256)
        src_v = src_rows[edges]
        scaled = src_v * rel_rows[edges]
        dst_v = dot(pick_dst[edges], slab[...])
        neg_v = dot(pick_neg[edges], slab[...]).astype(BF16)
        positive = jnp.sum(scaled * dst_v, axis=1, keepdims=True)
        pull = -jax.nn.sigmoid(-positive)
        pos_grad[edges] = pull
        scaled_b = scaled.astype(BF16)
        from_neg = []
        for j in range(2):
            block = slice(j * 128, j * 128 + 128)
            s, n = scaled_b[block], neg_v[block]
            score = lax.dot_general(s, n, (((1,), (1,)), ((), ())), preferred_element_type=F32)
            push = (jax.nn.sigmoid(score) * (1.0 / 128.0)).astype(BF16)
            weight[k * 256 + j * 128 : k * 256 + j * 128 + 128] = push
            from_neg.append(dot(push, n))
        grad = pull * dst_v + jnp.concatenate(from_neg, axis=0)
        scaled_grad[edges] = grad
        split_halves(g_rel, edges, grad * src_v)


def dst_gradients(src_rows, rel_rows, pos_grad, weight, g_dst):
    for k in range(NX):
        edges = slice(k * 256, k * 256 + 256)
        scaled = src_rows[edges] * rel_rows[edges]
        scaled_b = scaled.astype(BF16)
        split(g_dst, edges, pos_grad[edges] * scaled)
        for j in range(2):
            push = weight[k * 256 + j * 128 : k * 256 + j * 128 + 128]
            value = lax.dot_general(
                push, scaled_b[j * 128 : j * 128 + 128], (((0,), (0,)), ((), ())), preferred_element_type=F32
            )
            split(g_dst, slice(1024 + k * 256 + j * 128, 1024 + k * 256 + j * 128 + 128), value)


def src_gradients(rel_rows, scaled_grad, g_src):
    for k in range(NX):
        edges = slice(k * 256, k * 256 + 256)
        split(g_src, edges, scaled_grad[edges] * rel_rows[edges])


def both_terms(h, g):
    both = dot(h, g)
    return both[:, 0:256] + both[:, 256:512]


def window_kernel(
    embed,
    relation,
    src,
    dst,
    rel,
    neg,
    counts,
    state,
    new_embed,
    new_state,
    dest_out,
    rel_out,
    slab,
    index,
    src_rows,
    rel_rows,
    hot_src,
    hot_dst,
    hot_rel,
    own,
    table,
    parts,
    loaded,
    live,
    packed,
    g_src,
    g_dst,
    g_rel,
    pick_dst,
    pick_neg,
    scaled_grad,
    pos_grad,
    weight,
    own_state,
    rel_far,
    rel_near,
    src_part,
    dst_part,
    rel_pair,
    src_pair,
    dst_pair,
    rel_xy,
    rel_z,
    src_x,
    dst_x,
    src_half,
    dst_half,
    src_y,
    dst_y,
    load_sem,
    idx_send,
    idx_recv,
    slab_send,
    slab_recv,
    send,
    recv,
    dst_send,
    dst_recv,
    pair_recv,
    xy_recv,
    z_recv,
    all_recv,
    far_send,
    far_recv,
    here,
):
    b, g, z, y, x, c = position()
    loads = [pltpu.make_async_copy(ref.at[0, 0], loaded.at[i], load_sem.at[i]) for i, ref in enumerate((src, dst, rel, neg))]
    loads.append(pltpu.make_async_copy(counts.at[0], live, load_sem.at[4]))
    load_own = pltpu.make_async_copy(embed, own, load_sem.at[5])
    load_table = pltpu.make_async_copy(relation, table, load_sem.at[6])
    load_state = pltpu.make_async_copy(state, own_state, load_sem.at[7])
    for copy in loads:
        copy.start()
    load_own.start()
    load_table.start()
    load_state.start()

    sibling = (b, g + 1 - 2 * c)
    turn = pairing(z, x)
    behind = (lax.rem(b + NB - turn, NB), g)
    wanted = [(s, pairing(z + s, x) == s, (lax.rem(b + s, NB), g)) for s in (3, 2, 1)]
    opposite = at(z, lax.rem(y + 4, NY), x, c)
    yh = lax.div(y, 4)
    mine = x * NY + y

    y_order = (4, 3, 5, 2, 6, 1, 7, 0)
    z_offsets = (8, 7, 9, 6, 10, 5, 11, 4, 12, 3, 13, 2, 14, 1, 15)

    def plane(dx, dy):
        px, py = lax.rem(x + dx, NX), lax.rem(y + dy, NY)
        return px * NY + py, at(z, py, px, c)

    def along_x(d):
        return at(z, y, lax.rem(x + d, NX), c)

    def along_y(d):
        return at(z, lax.rem(y + NY + d, NY), x, c)

    def along_z(d):
        return at(lax.rem(z + NZ + d, NZ), y, x, c)

    def tell(i, *wheres):
        for where in wheres:
            pl.semaphore_signal(here.at[i], inc=1, device_id=where, device_id_type=MESH)

    greet(sibling)
    for d in (2, 1, 3):
        greet(along_x(d))
    for d in (1, -1):
        greet(along_y(d))
        greet(along_z(d))

    @pl.when(turn > 0)
    def _():
        greet(behind)

    for copy in loads:
        copy.wait()
    blocks = lax.broadcasted_iota(jnp.int32, (2, 128), 0)
    spots = lax.broadcasted_iota(jnp.int32, (1, 4), 1)
    for t in range(NX):
        count = jnp.sum(jnp.where(spots == t, live[...], 0), axis=1, keepdims=True)
        packed[t, 0] = jnp.where(blocks < count, loaded[0, t], -1)
        for i in range(1, 4):
            packed[t, i] = loaded[i, t]
    load_own.wait()
    pl.semaphore_wait(pltpu.get_barrier_semaphore(), 8 + sum(jnp.where(asked, 1, 0) for _, asked, _ in wanted))

    half = pl.ds(pl.multiple_of(c * 128, 128), 128)
    other = pl.ds(pl.multiple_of((1 - c) * 128, 128), 128)

    for s, asked, ahead in wanted:

        @pl.when(asked)
        def _():
            remote(own.at[half], slab.at[half], slab_send.at[s], slab_recv.at[0], ahead).start()

    sends = {}
    for d in (2, 1, 3):
        there = lax.rem(x + d, NX)
        sends[d] = remote(packed.at[pairing(z, there)], index.at[d], idx_send.at[d - 1], idx_recv.at[d - 1], along_x(d))
        sends[d].start()
    tell(0, along_y(1), along_y(-1))
    tell(1, along_z(1), along_z(-1))
    index[0:1] = packed[pl.ds(turn, 1)]

    @pl.when(turn == 0)
    def _():
        slab[...] = own[...]

    load_table.wait()
    r = table[...]
    high = r.astype(BF16)
    rest = r - high.astype(F32)
    middle = rest.astype(BF16)
    parts[:, 0:256] = high
    parts[:, 256:512] = middle
    parts[:, 512:768] = (rest - middle.astype(F32)).astype(BF16)

    lane = lax.broadcasted_iota(jnp.int32, (256, 256), 1)
    lane_r = lax.broadcasted_iota(jnp.int32, (256, 512), 1)
    sub = lax.broadcasted_iota(jnp.int32, (256, 256), 0)
    sub_r = lax.broadcasted_iota(jnp.int32, (2, 256, 256), 0) * 256 + lax.broadcasted_iota(jnp.int32, (2, 256, 256), 1)
    for k, d in enumerate((0, 1, 3, 2)):
        edges = slice(k * 256, k * 256 + 256)
        negs = slice(1024 + k * 256, 1024 + k * 256 + 256)
        if k == 1:
            pl.semaphore_wait(here.at[0], 2)
            pl.semaphore_wait(here.at[1], 2)
            tell(2, along_y(2), along_y(-2))
            tell(3, along_z(2), along_z(-2))
        if k == 2:
            pl.semaphore_wait(here.at[2], 2)
            pl.semaphore_wait(here.at[3], 2)
            tell(4, along_x(2), along_x(1), along_x(3))
            tell(5, along_z(4), along_z(-4))
        if k == 3:
            pl.semaphore_wait(here.at[4], 3)
            tell(6, along_z(-1), along_z(-2), along_z(-3))

        if d > 0:
            sends[d].wait_recv()
        src_rows[edges] = dot(hot(lane == columns_of(index[d, 0])), own[...])
        pieces = dot(hot(lane_r == columns_of(index[d, 2])), parts[...])
        rel_rows[edges] = (pieces[:, 0:256] + pieces[:, 256:512]) + pieces[:, 512:768]
        pick_dst[edges] = hot(lane == columns_of(index[d, 1]))
        pick_neg[edges] = hot(lane == columns_of(index[d, 3]))
        hot_src[:, edges] = hot(sub == line_of(index[d, 0]))
        hot_dst[:, edges] = hot(sub == line_of(index[d, 1]))
        hot_dst[:, negs] = hot(sub == line_of(index[d, 3]))
        hot_rel[:, :, edges] = hot(sub_r == line_of(index[d, 2])[None])

    @pl.when(turn > 0)
    def _():
        second = remote(slab.at[half], slab.at[half], slab_send.at[0], slab_recv.at[1], sibling)
        remote(own.at[half], slab.at[half], slab_send.at[0], slab_recv.at[0], sibling).wait_recv()
        second.start()
        remote(slab.at[other], slab.at[other], slab_send.at[0], slab_recv.at[1], sibling).wait_recv()
        second.wait_send()

    edge_gradients(slab, src_rows, rel_rows, pick_dst, pick_neg, scaled_grad, pos_grad, weight, g_rel)
    def pair(source, target, i):
        return remote(source, target, send.at[i], recv.at[i], sibling)

    def chunks(n, sem):
        return pltpu.make_async_copy(rel_xy.at[0, pl.ds(0, n)], rel_xy.at[0, pl.ds(0, n)], sem)

    def half_terms(core, h):
        both = dot(hot_rel[pl.ds(core, 1)][0], g_rel[:, 256 * h : 256 * h + 256])
        return (both[:, 0:128] + both[:, 128:256]).reshape(32, 8, 128)

    src_c = pair(src_part.at[:, :, 1 - c], src_pair, 1)
    dst_c = pair(dst_part.at[:, :, 1 - c], dst_pair, 2)
    offsets = [(dx, dy) for dx in (2, 1, 3, 0) for dy in y_order if (dx, dy) != (0, 0)]

    rel_c = [remote(rel_far.at[h], rel_pair.at[h], send.at[0], pair_recv.at[h], sibling) for h in range(2)]
    for h in range(2):
        rel_far[h] = half_terms(1 - c, h)
        rel_c[h].start()
    for h in range(2):
        rel_near[h] = half_terms(c, h)
    rel_c[0].wait_recv()
    rel_near[0] = rel_near[0] + rel_pair[0]
    for i, (dx, dy) in enumerate(offsets):
        chunk, where = plane(dx, dy)
        remote(rel_near.at[0, chunk], rel_xy.at[0, i], send.at[3], xy_recv.at[0], where).start()
    dst_gradients(src_rows, rel_rows, pos_grad, weight, g_dst)
    dst_part[...] = both_terms(hot_dst[...], g_dst[...]).reshape(2, 4, 2, 16, 256)
    dst_c.start()
    rel_c[1].wait_recv()
    rel_near[1] = rel_near[1] + rel_pair[1]
    for i, (dx, dy) in enumerate(offsets):
        chunk, where = plane(dx, dy)
        remote(rel_near.at[1, chunk], rel_xy.at[1, i], send.at[3], xy_recv.at[1], where).start()

    dst_c.wait_recv()
    dst_pair[...] = dst_pair[...] + dst_part[:, :, pl.ds(c, 1)].reshape(2, 4, 16, 256)

    past = z + 3 - turn >= NZ
    stays = jnp.logical_not(past)
    step_lo = lax.rem(lax.rem(y, 4) + 1, 4)
    to_rows = [remote(dst_pair.at[i], dst_y.at[yh], far_send.at[i], far_recv.at[yh], at(z, i * 4 + step_lo, x, c)) for i in range(2)]
    to_opposite = remote(dst_pair.at[1 - yh], dst_y.at[yh], far_send.at[0], far_recv.at[yh], opposite)

    def arrived(i):
        remote(dst_pair.at[0], dst_y.at[i], far_send.at[0], far_recv.at[i], opposite).wait_recv()

    src_gradients(rel_rows, scaled_grad, g_src)
    src_part[...] = both_terms(hot_src[...], g_src[...]).reshape(2, 4, 2, 16, 256)
    src_c.start()

    pl.semaphore_wait(here.at[5], 2)
    for h in range(2):
        chunks(31, xy_recv.at[h]).wait()
        rel_z[h, pl.ds(z, 1)] = (rel_near[h, pl.ds(mine, 1)][0] + jnp.sum(rel_xy[h], axis=0))[None]
        if h == 0:

            @pl.when(past)
            def _():
                to_rows[0].start()
                to_rows[1].start()

            @pl.when(stays)
            def _():
                to_opposite.start()

        for dz in z_offsets:
            remote(rel_z.at[h, z], rel_z.at[h, z], send.at[8], z_recv.at[h], along_z(dz)).start()

    src_c.wait_recv()
    src_pair[...] = src_pair[...] + src_part[:, :, pl.ds(c, 1)].reshape(2, 4, 16, 256)
    src_sends = []
    for d in (2, 1, 3):
        px = lax.rem(x + d, NX)
        copy = remote(src_pair.at[:, px], src_x.at[d], send.at[4 + d], recv.at[4 + d], at(z, y, px, c))
        copy.start()
        src_sends.append(copy)

    @pl.when(past)
    def _():
        arrived(0)
        arrived(1)
        dst_half[...] = dst_y[0] + dst_y[1]

    @pl.when(stays)
    def _():
        arrived(1 - yh)
        dst_half[...] = dst_pair[pl.ds(yh, 1)][0] + dst_y[pl.ds(1 - yh, 1)][0]

    pl.semaphore_wait(here.at[6], 3)
    for px in range(NX):
        to = at(lax.rem(z + 3 - turn, NZ), y, px, c)

        @pl.when(jnp.logical_or(turn != 3, x != px))
        def _():
            remote(dst_half.at[px], dst_x.at[turn], dst_send.at[px], dst_recv.at[turn], to).start()

    @pl.when(turn == 3)
    def _():
        dst_x[3:4] = dst_half[pl.ds(x, 1)]

    for copy in src_sends:
        copy.wait_recv()
    src_half[...] = (src_pair[:, pl.ds(x, 1)].reshape(2, 16, 256) + src_x[1]) + (src_x[2] + src_x[3])
    src_far = remote(src_half.at[1 - yh], src_y, send.at[9], recv.at[9], opposite)
    src_far.start()

    for h in range(2):
        cols = slice(128 * h, 128 * h + 128)
        chunks(15, z_recv.at[h]).wait()
        rel_out[pl.ds(c, 1), pl.ds(mine, 1), :, cols] = jnp.sum(rel_z[h], axis=0)[None, None]
        for dx, dy in offsets:
            _, where = plane(dx, dy)
            out = rel_out.at[c, mine, :, cols]
            remote(out, out, send.at[11], all_recv.at[h, dx], where).start()

    load_state.wait()
    src_far.wait_recv()
    total = src_half[pl.ds(yh, 1)][0] + src_y[...]
    lane = lax.broadcasted_iota(jnp.int32, (16, 256), 1)
    line = lax.broadcasted_iota(jnp.int32, (16, 256), 0)
    old = jnp.sum(jnp.where(lane == line + g * 16, own_state[...], 0.0), axis=1, keepdims=True)
    fresh = old + jnp.sum(total * total, axis=1, keepdims=True) * (1.0 / 256.0)
    new_embed[...] = own[pl.ds(pl.multiple_of(g * 16, 16), 16)].astype(F32) - 0.5 * total / jnp.sqrt(fresh)
    lane16 = lax.broadcasted_iota(jnp.int32, (16, 16), 1)
    line16 = lax.broadcasted_iota(jnp.int32, (16, 16), 0)
    new_state[...] = jnp.sum(jnp.where(lane16 == line16, fresh, 0.0), axis=0, keepdims=True)

    for h in range(2):
        for dx in (0, 1, 3, 2):
            chunks(7 if dx == 0 else 8, all_recv.at[h, dx]).wait()
            group = rel_out.at[c, pl.ds(lax.rem(x + NX - dx, NX) * NY, NY), :, 128 * h : 128 * h + 128]
            remote(group, group, send.at[12], recv.at[12], sibling).start()
    for t in range(NX):

        @pl.when(jnp.logical_or(turn != 3, t != 3))
        def _():
            remote(dst_half.at[t], dst_x.at[t], dst_send.at[t], dst_recv.at[t], sibling).wait_recv()

    dest_out[...] = (dst_x[0] + dst_x[1]) + (dst_x[2] + dst_x[3])
    for d in (1, 2, 3):
        sends[d].wait_send()
    for s, asked, ahead in wanted:

        @pl.when(asked)
        def _():
            remote(own.at[half], slab.at[half], slab_send.at[s], slab_recv.at[0], ahead).wait_send()

    remote(rel_far, rel_pair, send.at[0], recv.at[0], sibling).wait_send()
    src_c.wait_send()
    dst_c.wait_send()
    for _ in range(2):
        chunks(31, send.at[3]).wait()
        chunks(15, send.at[8]).wait()
        chunks(31, send.at[11]).wait()
    for copy in src_sends:
        copy.wait_send()
    for px in range(NX):

        @pl.when(jnp.logical_or(turn != 3, x != px))
        def _():
            remote(dst_half.at[px], dst_x.at[0], dst_send.at[px], dst_recv.at[0], sibling).wait_send()

    src_far.wait_send()

    @pl.when(past)
    def _():
        to_rows[0].wait_send()
        to_rows[1].wait_send()

    @pl.when(stays)
    def _():
        to_opposite.wait_send()

    last = remote(rel_out.at[c], rel_out.at[c], send.at[12], recv.at[12], sibling)
    last.wait_send()
    remote(rel_out.at[1 - c], rel_out.at[1 - c], send.at[12], recv.at[12], sibling).wait_recv()


def finish_kernel(a, b, c, d, a_out, b_out, c_out, d_out, sem):
    copies = [
        pltpu.make_async_copy(held, out, sem.at[i])
        for i, (held, out) in enumerate(((d, d_out), (a, a_out), (c, c_out), (b, b_out)))
    ]
    for copy in copies:
        copy.start()
    for copy in copies:
        copy.wait()


def on_device(embed, state, relation, src_index, dst_index, rel_index, neg_index, counts):
    vmem = pl.BlockSpec(memory_space=pltpu.VMEM)
    hbm = pl.BlockSpec(memory_space=pltpu.HBM)
    dma = pltpu.SemaphoreType.DMA

    def held(dims, kind=F32):
        return pltpu.VMEM(dims, kind)

    results = [
        jax.ShapeDtypeStruct(dims, F32) for dims in ((16, 256), (1, 16), (16, 256), (2, 32, 8, 256))
    ]
    given = (embed, relation, src_index, dst_index, rel_index, neg_index, counts, state.reshape(1, 256))
    found = pl.pallas_call(
        window_kernel,
        out_shape=results,
        in_specs=[hbm] * 8,
        out_specs=[vmem] * 4,
        scratch_shapes=[
            held((256, 256), BF16),
            held((4, 4, 2, 128), jnp.int32),
            held((1024, 256)),
            held((1024, 256)),
            held((256, 1024), BF16),
            held((256, 2048), BF16),
            held((2, 256, 1024), BF16),
            held((256, 256), BF16),
            held((512, 256)),
            held((512, 768), BF16),
            held((4, 4, 2, 128), jnp.int32),
            held((1, 4), jnp.int32),
            held((4, 4, 2, 128), jnp.int32),
            held((1024, 512), BF16),
            held((2048, 512), BF16),
            held((1024, 512), BF16),
            held((1024, 256), BF16),
            held((1024, 256), BF16),
            held((1024, 256)),
            held((1024, 1)),
            held((1024, 128), BF16),
            held((1, 256)),
            held((2, 32, 8, 128)),
            held((2, 32, 8, 128)),
            held((2, 4, 2, 16, 256)),
            held((2, 4, 2, 16, 256)),
            held((2, 32, 8, 128)),
            held((2, 4, 16, 256)),
            held((2, 4, 16, 256)),
            held((2, 31, 8, 128)),
            held((2, 16, 8, 128)),
            held((4, 2, 16, 256)),
            held((4, 16, 256)),
            held((2, 16, 256)),
            held((4, 16, 256)),
            held((16, 256)),
            held((2, 4, 16, 256)),
            dma((8,)),
            dma((3,)),
            dma((3,)),
            dma((4,)),
            dma((2,)),
            dma((13,)),
            dma((13,)),
            dma((4,)),
            dma((4,)),
            dma((2,)),
            dma((2,)),
            dma((2,)),
            dma((2, 4)),
            dma((2,)),
            dma((2,)),
            pltpu.SemaphoreType.REGULAR((7,)),
        ],
        compiler_params=pltpu.CompilerParams(
            vmem_limit_bytes=48 << 20, collective_id=0, has_side_effects=True
        ),
        name="window",
    )(*(pltpu.with_memory_space_constraint(a, pltpu.HBM) for a in given))
    new_embed, new_state, dest, rel_grad = pl.pallas_call(
        finish_kernel,
        out_shape=results,
        in_specs=[vmem] * 4,
        out_specs=[hbm] * 4,
        scratch_shapes=[dma((4,))],
        compiler_params=pltpu.CompilerParams(vmem_limit_bytes=4 << 20),
        name="finish",
    )(*found)
    return (new_embed, new_state.reshape(16), dest, rel_grad.reshape(512, 256))


def solution(mesh):
    return jax.shard_map(
        on_device,
        mesh=mesh,
        in_specs=(
            P("blk", None),
            P("blk"),
            P(),
            P("blk", "grp", None, None, None),
            P("blk", "grp", None, None, None),
            P("blk", "grp", None, None, None),
            P("blk", "grp", None, None, None),
            P("blk", "grp", None),
        ),
        out_specs=(P(("blk", "grp"), None), P(("blk", "grp")), P(("blk", "grp"), None), P()),
        check_vma=False,
    )
```

```python
import jax
import jax.numpy as jnp
from jax import lax
from jax.experimental import pallas as pl
from jax.experimental.pallas import tpu as pltpu
from jax.sharding import PartitionSpec as P

NZ = 16
NX = 4
NY = 8
NB = 64
MESH = pl.DeviceIdType.MESH
F32 = jnp.float32
BF16 = jnp.bfloat16


def position():
    b = lax.axis_index("blk")
    g = lax.axis_index("grp")
    z = lax.rem(b, NZ)
    y = lax.div(g, 8) * 4 + lax.div(b, NZ)
    x = lax.rem(lax.div(g, 2), NX)
    c = lax.rem(g, 2)
    return b, g, z, y, x, c


def at(z, y, x, c):
    return (lax.rem(y, 4) * NZ + z, lax.div(y, 4) * 8 + x * 2 + c)


def pairing(z, x):
    return x + lax.rem(z, 2) * (3 - 2 * x)


def remote(src, dst, send, recv, where):
    return pltpu.make_async_remote_copy(
        src_ref=src, dst_ref=dst, send_sem=send, recv_sem=recv, device_id=where, device_id_type=MESH
    )


def greet(where):
    pl.semaphore_signal(pltpu.get_barrier_semaphore(), inc=1, device_id=where, device_id_type=MESH)


def dot(a, b):
    return jnp.dot(a, b, preferred_element_type=F32)


def hot(hit):
    return jnp.where(hit, 1.0, 0.0).astype(BF16)


def columns_of(rows):
    turned = rows.T
    return jnp.concatenate([turned[:, 0:1], turned[:, 1:2]], axis=0)


def line_of(rows):
    return jnp.concatenate([rows[0:1], rows[1:2]], axis=1)


def split(ref, rows, value):
    top = value.astype(BF16)
    ref[rows, 0:256] = top
    ref[rows, 256:512] = (value - top.astype(F32)).astype(BF16)


def split_halves(ref, rows, value):
    top = value.astype(BF16)
    low = (value - top.astype(F32)).astype(BF16)
    for h in range(2):
        ref[rows, 256 * h : 256 * h + 128] = top[:, 128 * h : 128 * h + 128]
        ref[rows, 256 * h + 128 : 256 * h + 256] = low[:, 128 * h : 128 * h + 128]


def edge_gradients(slab, src_rows, rel_rows, pick_dst, pick_neg, scaled_grad, pos_grad, weight, g_rel):
    for k in range(NX):
        edges = slice(k * 256, k * 256 + 256)
        src_v = src_rows[edges]
        scaled = src_v * rel_rows[edges]
        dst_v = dot(pick_dst[edges], slab[...])
        neg_v = dot(pick_neg[edges], slab[...]).astype(BF16)
        positive = jnp.sum(scaled * dst_v, axis=1, keepdims=True)
        pull = -jax.nn.sigmoid(-positive)
        pos_grad[edges] = pull
        scaled_b = scaled.astype(BF16)
        from_neg = []
        for j in range(2):
            block = slice(j * 128, j * 128 + 128)
            s, n = scaled_b[block], neg_v[block]
            score = lax.dot_general(s, n, (((1,), (1,)), ((), ())), preferred_element_type=F32)
            push = (jax.nn.sigmoid(score) * (1.0 / 128.0)).astype(BF16)
            weight[k * 256 + j * 128 : k * 256 + j * 128 + 128] = push
            from_neg.append(dot(push, n))
        grad = pull * dst_v + jnp.concatenate(from_neg, axis=0)
        scaled_grad[edges] = grad
        split_halves(g_rel, edges, grad * src_v)


def dst_gradients(src_rows, rel_rows, pos_grad, weight, g_dst):
    for k in range(NX):
        edges = slice(k * 256, k * 256 + 256)
        scaled = src_rows[edges] * rel_rows[edges]
        scaled_b = scaled.astype(BF16)
        split(g_dst, edges, pos_grad[edges] * scaled)
        for j in range(2):
            push = weight[k * 256 + j * 128 : k * 256 + j * 128 + 128]
            value = lax.dot_general(
                push, scaled_b[j * 128 : j * 128 + 128], (((0,), (0,)), ((), ())), preferred_element_type=F32
            )
            split(g_dst, slice(1024 + k * 256 + j * 128, 1024 + k * 256 + j * 128 + 128), value)


def src_gradients(rel_rows, scaled_grad, g_src):
    for k in range(NX):
        edges = slice(k * 256, k * 256 + 256)
        split(g_src, edges, scaled_grad[edges] * rel_rows[edges])


def both_terms(h, g):
    both = dot(h, g)
    return both[:, 0:256] + both[:, 256:512]


def window_kernel(
    embed,
    relation,
    src,
    dst,
    rel,
    neg,
    counts,
    state,
    new_embed,
    new_state,
    dest_out,
    rel_out,
    slab,
    index,
    src_rows,
    rel_rows,
    hot_src,
    hot_dst,
    hot_rel,
    own,
    table,
    parts,
    loaded,
    live,
    packed,
    g_src,
    g_dst,
    g_rel,
    pick_dst,
    pick_neg,
    scaled_grad,
    pos_grad,
    weight,
    own_state,
    rel_far,
    rel_near,
    src_part,
    dst_part,
    rel_pair,
    src_pair,
    dst_pair,
    rel_xy,
    rel_z,
    src_x,
    dst_x,
    src_half,
    dst_half,
    src_y,
    dst_y,
    load_sem,
    idx_send,
    idx_recv,
    slab_send,
    slab_recv,
    send,
    recv,
    dst_send,
    dst_recv,
    pair_recv,
    xy_recv,
    z_recv,
    all_recv,
    far_send,
    far_recv,
    here,
):
    b, g, z, y, x, c = position()
    loads = [pltpu.make_async_copy(ref.at[0, 0], loaded.at[i], load_sem.at[i]) for i, ref in enumerate((src, dst, rel, neg))]
    loads.append(pltpu.make_async_copy(counts.at[0], live, load_sem.at[4]))
    load_own = pltpu.make_async_copy(embed, own, load_sem.at[5])
    load_table = pltpu.make_async_copy(relation, table, load_sem.at[6])
    load_state = pltpu.make_async_copy(state, own_state, load_sem.at[7])

    sibling = (b, g + 1 - 2 * c)
    turn = pairing(z, x)
    behind = (lax.rem(b + NB - turn, NB), g)
    wanted = [(s, pairing(z + s, x) == s, (lax.rem(b + s, NB), g)) for s in (3, 2, 1)]
    opposite = at(z, lax.rem(y + 4, NY), x, c)
    yh = lax.div(y, 4)
    mine = x * NY + y

    y_order = (4, 3, 5, 2, 6, 1, 7, 0)
    z_offsets = (8, 7, 9, 6, 10, 5, 11, 4, 12, 3, 13, 2, 14, 1, 15)

    def plane(dx, dy):
        px, py = lax.rem(x + dx, NX), lax.rem(y + dy, NY)
        return px * NY + py, at(z, py, px, c)

    def along_x(d):
        return at(z, y, lax.rem(x + d, NX), c)

    def along_y(d):
        return at(z, lax.rem(y + NY + d, NY), x, c)

    def along_z(d):
        return at(lax.rem(z + NZ + d, NZ), y, x, c)

    def tell(i, *wheres):
        for where in wheres:
            pl.semaphore_signal(here.at[i], inc=1, device_id=where, device_id_type=MESH)

    greet(sibling)
    for d in (2, 1, 3):
        greet(along_x(d))
    for d in (1, -1):
        greet(along_y(d))
        greet(along_z(d))

    @pl.when(turn > 0)
    def _():
        greet(behind)

    for copy in loads:
        copy.start()
    load_own.start()
    load_table.start()
    load_state.start()

    for copy in loads:
        copy.wait()
    blocks = lax.broadcasted_iota(jnp.int32, (2, 128), 0)
    spots = lax.broadcasted_iota(jnp.int32, (1, 4), 1)
    for t in range(NX):
        count = jnp.sum(jnp.where(spots == t, live[...], 0), axis=1, keepdims=True)
        packed[t, 0] = jnp.where(blocks < count, loaded[0, t], -1)
        for i in range(1, 4):
            packed[t, i] = loaded[i, t]
    load_own.wait()
    pl.semaphore_wait(pltpu.get_barrier_semaphore(), 8 + sum(jnp.where(asked, 1, 0) for _, asked, _ in wanted))

    half = pl.ds(pl.multiple_of(c * 128, 128), 128)
    other = pl.ds(pl.multiple_of((1 - c) * 128, 128), 128)

    for s, asked, ahead in wanted:

        @pl.when(asked)
        def _():
            remote(own.at[half], slab.at[half], slab_send.at[s], slab_recv.at[0], ahead).start()

    sends = {}
    for d in (2, 1, 3):
        there = lax.rem(x + d, NX)
        sends[d] = remote(packed.at[pairing(z, there)], index.at[d], idx_send.at[d - 1], idx_recv.at[d - 1], along_x(d))
        sends[d].start()
    tell(0, along_y(1), along_y(-1))
    tell(1, along_z(1), along_z(-1))
    index[0:1] = packed[pl.ds(turn, 1)]

    @pl.when(turn == 0)
    def _():
        slab[...] = own[...]

    load_table.wait()
    r = table[...]
    high = r.astype(BF16)
    rest = r - high.astype(F32)
    middle = rest.astype(BF16)
    parts[:, 0:256] = high
    parts[:, 256:512] = middle
    parts[:, 512:768] = (rest - middle.astype(F32)).astype(BF16)

    lane = lax.broadcasted_iota(jnp.int32, (256, 256), 1)
    lane_r = lax.broadcasted_iota(jnp.int32, (256, 512), 1)
    sub = lax.broadcasted_iota(jnp.int32, (256, 256), 0)
    sub_r = lax.broadcasted_iota(jnp.int32, (2, 256, 256), 0) * 256 + lax.broadcasted_iota(jnp.int32, (2, 256, 256), 1)
    for k, d in enumerate((0, 1, 3, 2)):
        edges = slice(k * 256, k * 256 + 256)
        negs = slice(1024 + k * 256, 1024 + k * 256 + 256)
        if k == 1:
            pl.semaphore_wait(here.at[0], 2)
            pl.semaphore_wait(here.at[1], 2)
            tell(2, along_y(2), along_y(-2))
            tell(3, along_z(2), along_z(-2))
        if k == 2:
            pl.semaphore_wait(here.at[2], 2)
            pl.semaphore_wait(here.at[3], 2)
            tell(4, along_x(2), along_x(1), along_x(3))
            tell(5, along_z(4), along_z(-4))
        if k == 3:
            pl.semaphore_wait(here.at[4], 3)
            tell(6, along_z(-1), along_z(-2), along_z(-3))

        if d > 0:
            sends[d].wait_recv()
        src_rows[edges] = dot(hot(lane == columns_of(index[d, 0])), own[...])
        pieces = dot(hot(lane_r == columns_of(index[d, 2])), parts[...])
        rel_rows[edges] = (pieces[:, 0:256] + pieces[:, 256:512]) + pieces[:, 512:768]
        pick_dst[edges] = hot(lane == columns_of(index[d, 1]))
        pick_neg[edges] = hot(lane == columns_of(index[d, 3]))
        hot_src[:, edges] = hot(sub == line_of(index[d, 0]))
        hot_dst[:, edges] = hot(sub == line_of(index[d, 1]))
        hot_dst[:, negs] = hot(sub == line_of(index[d, 3]))
        hot_rel[:, :, edges] = hot(sub_r == line_of(index[d, 2])[None])

    @pl.when(turn > 0)
    def _():
        second = remote(slab.at[half], slab.at[half], slab_send.at[0], slab_recv.at[1], sibling)
        remote(own.at[half], slab.at[half], slab_send.at[0], slab_recv.at[0], sibling).wait_recv()
        second.start()
        remote(slab.at[other], slab.at[other], slab_send.at[0], slab_recv.at[1], sibling).wait_recv()
        second.wait_send()

    edge_gradients(slab, src_rows, rel_rows, pick_dst, pick_neg, scaled_grad, pos_grad, weight, g_rel)
    def pair(source, target, i):
        return remote(source, target, send.at[i], recv.at[i], sibling)

    def chunks(n, sem):
        return pltpu.make_async_copy(rel_xy.at[0, pl.ds(0, n)], rel_xy.at[0, pl.ds(0, n)], sem)

    def half_terms(core, h):
        both = dot(hot_rel[pl.ds(core, 1)][0], g_rel[:, 256 * h : 256 * h + 256])
        return (both[:, 0:128] + both[:, 128:256]).reshape(32, 8, 128)

    src_c = pair(src_part.at[:, :, 1 - c], src_pair, 1)
    dst_c = pair(dst_part.at[:, :, 1 - c], dst_pair, 2)
    offsets = [(dx, dy) for dx in (2, 1, 3, 0) for dy in y_order if (dx, dy) != (0, 0)]

    rel_c = [remote(rel_far.at[h], rel_pair.at[h], send.at[0], pair_recv.at[h], sibling) for h in range(2)]
    for h in range(2):
        rel_far[h] = half_terms(1 - c, h)
        rel_c[h].start()
    rel_near[0] = half_terms(c, 0)
    rel_c[0].wait_recv()
    rel_near[0] = rel_near[0] + rel_pair[0]
    for i, (dx, dy) in enumerate(offsets):
        chunk, where = plane(dx, dy)
        remote(rel_near.at[0, chunk], rel_xy.at[0, i], send.at[3], xy_recv.at[0], where).start()
    dst_gradients(src_rows, rel_rows, pos_grad, weight, g_dst)
    dst_part[...] = both_terms(hot_dst[...], g_dst[...]).reshape(2, 4, 2, 16, 256)
    dst_c.start()
    rel_near[1] = half_terms(c, 1)
    rel_c[1].wait_recv()
    rel_near[1] = rel_near[1] + rel_pair[1]
    for i, (dx, dy) in enumerate(offsets):
        chunk, where = plane(dx, dy)
        remote(rel_near.at[1, chunk], rel_xy.at[1, i], send.at[3], xy_recv.at[1], where).start()

    dst_c.wait_recv()
    dst_pair[...] = dst_pair[...] + dst_part[:, :, pl.ds(c, 1)].reshape(2, 4, 16, 256)

    past = z + 3 - turn >= NZ
    stays = jnp.logical_not(past)
    step_lo = lax.rem(lax.rem(y, 4) + 1, 4)
    to_rows = [remote(dst_pair.at[i], dst_y.at[yh], far_send.at[i], far_recv.at[yh], at(z, i * 4 + step_lo, x, c)) for i in range(2)]
    to_opposite = remote(dst_pair.at[1 - yh], dst_y.at[yh], far_send.at[0], far_recv.at[yh], opposite)

    def arrived(i):
        remote(dst_pair.at[0], dst_y.at[i], far_send.at[0], far_recv.at[i], opposite).wait_recv()

    src_gradients(rel_rows, scaled_grad, g_src)
    src_part[...] = both_terms(hot_src[...], g_src[...]).reshape(2, 4, 2, 16, 256)
    src_c.start()

    pl.semaphore_wait(here.at[5], 2)
    for h in range(2):
        chunks(31, xy_recv.at[h]).wait()
        rel_z[h, pl.ds(z, 1)] = (rel_near[h, pl.ds(mine, 1)][0] + jnp.sum(rel_xy[h], axis=0))[None]
        if h == 0:

            @pl.when(past)
            def _():
                to_rows[0].start()
                to_rows[1].start()

            @pl.when(stays)
            def _():
                to_opposite.start()

        for dz in z_offsets:
            remote(rel_z.at[h, z], rel_z.at[h, z], send.at[8], z_recv.at[h], along_z(dz)).start()

    src_c.wait_recv()
    src_pair[...] = src_pair[...] + src_part[:, :, pl.ds(c, 1)].reshape(2, 4, 16, 256)
    src_sends = []
    for d in (2, 1, 3):
        px = lax.rem(x + d, NX)
        copy = remote(src_pair.at[:, px], src_x.at[d], send.at[4 + d], recv.at[4 + d], at(z, y, px, c))
        copy.start()
        src_sends.append(copy)

    @pl.when(past)
    def _():
        arrived(0)
        arrived(1)
        dst_half[...] = dst_y[0] + dst_y[1]

    @pl.when(stays)
    def _():
        arrived(1 - yh)
        dst_half[...] = dst_pair[pl.ds(yh, 1)][0] + dst_y[pl.ds(1 - yh, 1)][0]

    pl.semaphore_wait(here.at[6], 3)
    for px in range(NX):
        to = at(lax.rem(z + 3 - turn, NZ), y, px, c)

        @pl.when(jnp.logical_or(turn != 3, x != px))
        def _():
            remote(dst_half.at[px], dst_x.at[turn], dst_send.at[px], dst_recv.at[turn], to).start()

    @pl.when(turn == 3)
    def _():
        dst_x[3:4] = dst_half[pl.ds(x, 1)]

    for copy in src_sends:
        copy.wait_recv()
    src_half[...] = (src_pair[:, pl.ds(x, 1)].reshape(2, 16, 256) + src_x[1]) + (src_x[2] + src_x[3])
    src_far = remote(src_half.at[1 - yh], src_y, send.at[9], recv.at[9], opposite)
    src_far.start()

    for h in range(2):
        cols = slice(128 * h, 128 * h + 128)
        chunks(15, z_recv.at[h]).wait()
        rel_out[pl.ds(c, 1), pl.ds(mine, 1), :, cols] = jnp.sum(rel_z[h], axis=0)[None, None]
        for dx, dy in offsets:
            _, where = plane(dx, dy)
            out = rel_out.at[c, mine, :, cols]
            remote(out, out, send.at[11], all_recv.at[h, dx], where).start()

    load_state.wait()
    src_far.wait_recv()
    total = src_half[pl.ds(yh, 1)][0] + src_y[...]
    lane = lax.broadcasted_iota(jnp.int32, (16, 256), 1)
    line = lax.broadcasted_iota(jnp.int32, (16, 256), 0)
    old = jnp.sum(jnp.where(lane == line + g * 16, own_state[...], 0.0), axis=1, keepdims=True)
    fresh = old + jnp.sum(total * total, axis=1, keepdims=True) * (1.0 / 256.0)
    new_embed[...] = own[pl.ds(pl.multiple_of(g * 16, 16), 16)].astype(F32) - 0.5 * total / jnp.sqrt(fresh)
    lane16 = lax.broadcasted_iota(jnp.int32, (16, 16), 1)
    line16 = lax.broadcasted_iota(jnp.int32, (16, 16), 0)
    new_state[...] = jnp.sum(jnp.where(lane16 == line16, fresh, 0.0), axis=0, keepdims=True)

    for h in range(2):
        for dx in (0, 1, 3, 2):
            chunks(7 if dx == 0 else 8, all_recv.at[h, dx]).wait()
            group = rel_out.at[c, pl.ds(lax.rem(x + NX - dx, NX) * NY, NY), :, 128 * h : 128 * h + 128]
            remote(group, group, send.at[12], recv.at[12], sibling).start()
    for t in range(NX):

        @pl.when(jnp.logical_or(turn != 3, t != 3))
        def _():
            remote(dst_half.at[t], dst_x.at[t], dst_send.at[t], dst_recv.at[t], sibling).wait_recv()

    dest_out[...] = (dst_x[0] + dst_x[1]) + (dst_x[2] + dst_x[3])
    for d in (1, 2, 3):
        sends[d].wait_send()
    for s, asked, ahead in wanted:

        @pl.when(asked)
        def _():
            remote(own.at[half], slab.at[half], slab_send.at[s], slab_recv.at[0], ahead).wait_send()

    remote(rel_far, rel_pair, send.at[0], recv.at[0], sibling).wait_send()
    src_c.wait_send()
    dst_c.wait_send()
    for _ in range(2):
        chunks(31, send.at[3]).wait()
        chunks(15, send.at[8]).wait()
        chunks(31, send.at[11]).wait()
    for copy in src_sends:
        copy.wait_send()
    for px in range(NX):

        @pl.when(jnp.logical_or(turn != 3, x != px))
        def _():
            remote(dst_half.at[px], dst_x.at[0], dst_send.at[px], dst_recv.at[0], sibling).wait_send()

    src_far.wait_send()

    @pl.when(past)
    def _():
        to_rows[0].wait_send()
        to_rows[1].wait_send()

    @pl.when(stays)
    def _():
        to_opposite.wait_send()

    last = remote(rel_out.at[c], rel_out.at[c], send.at[12], recv.at[12], sibling)
    last.wait_send()
    remote(rel_out.at[1 - c], rel_out.at[1 - c], send.at[12], recv.at[12], sibling).wait_recv()


def finish_kernel(a, b, c, d, a_out, b_out, c_out, d_out, sem):
    copies = [
        pltpu.make_async_copy(held, out, sem.at[i])
        for i, (held, out) in enumerate(((d, d_out), (a, a_out), (c, c_out), (b, b_out)))
    ]
    for copy in copies:
        copy.start()
    for copy in copies:
        copy.wait()


def on_device(embed, state, relation, src_index, dst_index, rel_index, neg_index, counts):
    vmem = pl.BlockSpec(memory_space=pltpu.VMEM)
    hbm = pl.BlockSpec(memory_space=pltpu.HBM)
    dma = pltpu.SemaphoreType.DMA

    def held(dims, kind=F32):
        return pltpu.VMEM(dims, kind)

    results = [
        jax.ShapeDtypeStruct(dims, F32) for dims in ((16, 256), (1, 16), (16, 256), (2, 32, 8, 256))
    ]
    given = (embed, relation, src_index, dst_index, rel_index, neg_index, counts, state.reshape(1, 256))
    found = pl.pallas_call(
        window_kernel,
        out_shape=results,
        in_specs=[hbm] * 8,
        out_specs=[vmem] * 4,
        scratch_shapes=[
            held((256, 256), BF16),
            held((4, 4, 2, 128), jnp.int32),
            held((1024, 256)),
            held((1024, 256)),
            held((256, 1024), BF16),
            held((256, 2048), BF16),
            held((2, 256, 1024), BF16),
            held((256, 256), BF16),
            held((512, 256)),
            held((512, 768), BF16),
            held((4, 4, 2, 128), jnp.int32),
            held((1, 4), jnp.int32),
            held((4, 4, 2, 128), jnp.int32),
            held((1024, 512), BF16),
            held((2048, 512), BF16),
            held((1024, 512), BF16),
            held((1024, 256), BF16),
            held((1024, 256), BF16),
            held((1024, 256)),
            held((1024, 1)),
            held((1024, 128), BF16),
            held((1, 256)),
            held((2, 32, 8, 128)),
            held((2, 32, 8, 128)),
            held((2, 4, 2, 16, 256)),
            held((2, 4, 2, 16, 256)),
            held((2, 32, 8, 128)),
            held((2, 4, 16, 256)),
            held((2, 4, 16, 256)),
            held((2, 31, 8, 128)),
            held((2, 16, 8, 128)),
            held((4, 2, 16, 256)),
            held((4, 16, 256)),
            held((2, 16, 256)),
            held((4, 16, 256)),
            held((16, 256)),
            held((2, 4, 16, 256)),
            dma((8,)),
            dma((3,)),
            dma((3,)),
            dma((4,)),
            dma((2,)),
            dma((13,)),
            dma((13,)),
            dma((4,)),
            dma((4,)),
            dma((2,)),
            dma((2,)),
            dma((2,)),
            dma((2, 4)),
            dma((2,)),
            dma((2,)),
            pltpu.SemaphoreType.REGULAR((7,)),
        ],
        compiler_params=pltpu.CompilerParams(
            vmem_limit_bytes=48 << 20, collective_id=0, has_side_effects=True
        ),
        name="window",
    )(*(pltpu.with_memory_space_constraint(a, pltpu.HBM) for a in given))
    new_embed, new_state, dest, rel_grad = pl.pallas_call(
        finish_kernel,
        out_shape=results,
        in_specs=[vmem] * 4,
        out_specs=[hbm] * 4,
        scratch_shapes=[dma((4,))],
        compiler_params=pltpu.CompilerParams(vmem_limit_bytes=4 << 20),
        name="finish",
    )(*found)
    return (new_embed, new_state.reshape(16), dest, rel_grad.reshape(512, 256))


def solution(mesh):
    return jax.shard_map(
        on_device,
        mesh=mesh,
        in_specs=(
            P("blk", None),
            P("blk"),
            P(),
            P("blk", "grp", None, None, None),
            P("blk", "grp", None, None, None),
            P("blk", "grp", None, None, None),
            P("blk", "grp", None, None, None),
            P("blk", "grp", None),
        ),
        out_specs=(P(("blk", "grp"), None), P(("blk", "grp")), P(("blk", "grp"), None), P()),
        check_vma=False,
    )
```
